1024 devices in a mesh: grp: 8 (over y, core), rep: 128 (over z, x).
Axes of the slice: x: 4, y: 4, z: 32, core: 2. Of those that a mesh axis runs over, the one named last changes fastest.
Arguments:
- queries: bfloat16 [131072, 1024], P(('grp', 'rep')), may hold values from -0.5 to 0.5
- passages: bfloat16 [131072, 1024], P(('grp', 'rep')), may hold values from -0.5 to 0.5
- bank: bfloat16 [512, 1024], P('rep'), may hold values from -0.5 to 0.5
- hard_ids: int32 [131072, 7], P(('grp', 'rep')), may hold values from 0 to 511
- weights: float32 [131072], P(('grp', 'rep')), may hold values from 0.5 to 2
Outputs:
- losses: float32 [131072], P(('grp', 'rep'))
- query_grad: float32 [131072, 1024], P(('grp', 'rep'))
- passage_grad: float32 [131072, 1024], P(('grp', 'rep'))
- bank_grad: float32 [512, 1024], P('rep')
The draws below stay inside these ranges and needn't reach their ends.
Inputs may be any that keep to these rules, and one draw needn't show every extreme that they name: hard_ids[b, k] is a row of bank, held by index hard_ids[b, k] // 4 of rep; rows may repeat, and a few rows are named far more often than others.
All inputs are finite; a program needn't handle non-finite values.
Results may differ from the reference program's by a relative error of at most 0.0065.
The reference program's roundings to bfloat16 on the way count: a program that leaves them out, or rounds other values in their place, can miss the bound.
Values may be sent and summed in bfloat16 or wider, within the bound.
A program may use at most 32 MiB of HBM per device.

```python
import math
import jax
import jax.numpy as jnp
import numpy as np
from jax import lax

D = 1024
Q = 128
HARD = 7
BANK = 4
B = 131072
NB = 512
N_GRP = 8
N_REP = 128


def plant(drawn, key, least, high):
    extent = drawn.shape
    spot = [jax.random.randint(jax.random.fold_in(key, axis), (), 0, extent[axis]) for axis in range(len(extent))]
    drawn = drawn.at[tuple(spot)].set(least)
    longest = extent.index(max(extent))
    spot[longest] = (spot[longest] + 1) % extent[longest]
    return drawn.at[tuple(spot)].set(high)


def levels(own_key, dims, split, low, top_value):
    def one(position, shards_of):
        steps = jax.random.uniform(jax.random.fold_in(jax.random.fold_in(own_key, 6), position), (shards_of,), jnp.float32, low / len(split), top_value / len(split))
        return jnp.repeat(jnp.exp(steps), dims[position] // shards_of).reshape((-1,) + (1,) * (len(dims) - position - 1))

    factor_of = one(*split[0])
    for cut in split[1:]:
        factor_of = factor_of * one(*cut)
    return factor_of


def rank_bounds(amount, skew):
    weights = [(1 << 20) // math.isqrt(rank ** skew) + 1 for rank in range(1, amount + 1)]
    width = 1 + sum(weights) // (1 << 30)
    return np.cumsum(np.array([max(1, weight // width) for weight in weights]))


def ranked(key, shape, count, skew):
    table = rank_bounds(count, skew)
    pick = jax.random.randint(jax.random.fold_in(key, 1), shape, 0, int(table[count - 1]))
    rank = jnp.searchsorted(jnp.asarray(table, jnp.int32), pick, side="right")
    return jax.random.permutation(jax.random.fold_in(key, 2), count)[rank].astype(jnp.int32)


def normal_values(key, extent, width, limit, pieces=(), held_as=jnp.bfloat16):
    result = width * jax.random.normal(key, extent, jnp.float32)
    if pieces:
        result = result * levels(key, extent, pieces, -0.22, 0.18)
    return jnp.clip(result, -limit, limit).astype(held_as)


def setup_inputs(seed: int = 0) -> dict:
    splits = jax.random.split(jax.random.key(seed), 6)
    return {
        "queries": normal_values(splits[0], (B, D), 0.03125, 0.5, ((0, 1024),)),
        "passages": normal_values(splits[1], (B, D), 0.03125, 0.5, ((0, 1024),)),
        "bank": normal_values(splits[2], (NB, D), 0.03125, 0.5, ((0, 128),)),
        "hard_ids": plant(ranked(splits[3], (B, HARD), NB, 2), jax.random.fold_in(splits[3], 3), 0, NB - 1).astype(jnp.int32),
        "weights": jnp.clip(jnp.exp(math.log(2.0) - 1.3862944 * jax.random.uniform(splits[4], (B,), jnp.float32) ** levels(splits[4], (B,), ((0, 1024),), -0.2, 0.2)), 0.5, 2.0),
    }


logit_divisor_heat = 0.05
epsilon = 1e-06

def unit_rows(values):
    widened = values.astype(jnp.float32)
    inverse = 1.0 / jnp.sqrt(lax.optimization_barrier(jnp.sum(widened * widened, axis=-1, keepdims=True)) + epsilon)
    return (widened * inverse, inverse)

def unit_backward(unit_vec, inverse, upstream):
    return inverse * (upstream - unit_vec * lax.optimization_barrier(jnp.sum(unit_vec * upstream, axis=-1, keepdims=True)))

def contrast(search_latent_entries, document_cohort_entries, distractor_entries, sample_importance_list, positive):
    cohort_logit_table = jnp.dot(search_latent_entries, document_cohort_entries.T, preferred_element_type=jnp.float32) / logit_divisor_heat
    distractor_logit_table = jnp.einsum('ch,clh->cl', search_latent_entries, distractor_entries, preferred_element_type=jnp.float32) / logit_divisor_heat
    summed = lax.optimization_barrier(jnp.sum(jnp.exp(cohort_logit_table), axis=1)) + lax.optimization_barrier(jnp.sum(jnp.exp(distractor_logit_table), axis=1))
    log_total = jnp.log(summed)
    correct_pair_indicator = (jnp.arange(document_cohort_entries.shape[0], dtype=jnp.int32)[None, :] == positive[:, None]).astype(jnp.float32)
    losses = log_total - lax.optimization_barrier(jnp.sum(correct_pair_indicator * cohort_logit_table, axis=1))
    cohort_likelihood = jnp.exp(cohort_logit_table - log_total[:, None])
    distractor_likelihood = jnp.exp(distractor_logit_table - log_total[:, None])
    cohort_logit_slope = (sample_importance_list[:, None] * (cohort_likelihood - correct_pair_indicator) / logit_divisor_heat).astype(jnp.bfloat16)
    distractor_logit_slope = (sample_importance_list[:, None] * distractor_likelihood / logit_divisor_heat).astype(jnp.bfloat16)
    query_up = jnp.dot(cohort_logit_slope, document_cohort_entries, preferred_element_type=jnp.float32)
    query_up = query_up + jnp.einsum('mk,mkd->md', distractor_logit_slope, distractor_entries, preferred_element_type=jnp.float32)
    passage_up = jnp.dot(cohort_logit_slope.T, search_latent_entries, preferred_element_type=jnp.float32)
    return (losses, query_up, passage_up, distractor_logit_slope)

def bank_terms(row_ids, distractor_logit_slope, search_latent_entries, row_count):
    selector = (row_ids[:, :, None] == jnp.arange(row_count, dtype=jnp.int32)[None, None, :]).astype(jnp.bfloat16)
    weighted = (selector * distractor_logit_slope[:, :, None]).reshape(-1, row_count)
    repeated = jnp.broadcast_to(search_latent_entries[:, None, :], (row_ids.shape[0], row_ids.shape[1], search_latent_entries.shape[1])).reshape(-1, search_latent_entries.shape[1])
    return jnp.dot(weighted.T, repeated, preferred_element_type=jnp.float32)

def reference(queries, passages, bank, hard_ids, weights):
    query_unit, query_inverse = unit_rows(queries)
    passage_unit, passage_inverse = unit_rows(passages)
    bank_unit, bank_inverse = unit_rows(bank)
    search_latent_entries = query_unit.astype(jnp.bfloat16)
    passage_rows = passage_unit.astype(jnp.bfloat16)
    bank_rows = bank_unit.astype(jnp.bfloat16)
    members = N_GRP * Q
    row_count = BANK * N_REP

    def regroup(values):
        shaped = values.reshape((N_GRP, N_REP, Q) + values.shape[1:])
        return jnp.swapaxes(shaped, 0, 1).reshape((N_REP, members) + values.shape[1:])

    def ungroup(values):
        shaped = values.reshape((N_REP, N_GRP, Q) + values.shape[2:])
        return jnp.swapaxes(shaped, 0, 1).reshape((N_GRP * N_REP * Q,) + values.shape[2:])
    positive = jnp.arange(members, dtype=jnp.int32)

    def group_step(running, inputs):
        group_queries, group_passages, group_ids, group_weights = inputs
        distractor_entries = bank_rows[group_ids]
        losses, query_up, passage_up, distractor_logit_slope = contrast(group_queries, group_passages, distractor_entries, group_weights, positive)
        running = running + bank_terms(group_ids, distractor_logit_slope, group_queries, row_count)
        return (running, (losses, query_up, passage_up))
    initial = jnp.zeros((row_count, D), jnp.float32)
    bank_up, (losses, query_up, passage_up) = lax.scan(group_step, initial, (regroup(search_latent_entries), regroup(passage_rows), regroup(hard_ids), regroup(weights)))
    query_grad = unit_backward(query_unit, query_inverse, ungroup(query_up))
    passage_grad = unit_backward(passage_unit, passage_inverse, ungroup(passage_up))
    bank_grad = unit_backward(bank_unit, bank_inverse, bank_up)
    return (ungroup(losses), query_grad, passage_grad, bank_grad)
```

```python
import functools

import jax
import jax.numpy as jnp
from jax import lax
from jax.experimental import pallas as pl
from jax.experimental.pallas import tpu as pltpu
from jax.sharding import PartitionSpec as P

MESH = pl.DeviceIdType.MESH
F32 = jnp.float32
BF16 = jnp.bfloat16
EPS = 1e-06
HEAT = 20.0
NX = 4
GROUP = 8
ROW_OF = [2 * ((m >> 2 & 1) ^ (m >> 1 & 1)) + (m & 1) for m in range(GROUP)]


def dot_nt(left, right):
    return lax.dot_general(left, right, (((1,), (1,)), ((), ())), preferred_element_type=F32)


def dot_tn(left, right):
    return lax.dot_general(left, right, (((0,), (0,)), ((), ())), preferred_element_type=F32)


def dot_nn(left, right):
    return jnp.dot(left, right, preferred_element_type=F32)


def kernel(
    nz,
    nx,
    q_in,
    p_in,
    bank_in,
    ids_in,
    w_in,
    loss_out,
    qg_out,
    pg_out,
    bg_out,
    q_raw,
    p_raw,
    bank_raw,
    meta_raw,
    w_raw,
    rows_q,
    cols,
    bank_x,
    own_row,
    gathered,
    wide,
    meta,
    sums,
    e_t,
    g_t,
    bank_out,
    plane_in,
    z_out,
    z_in,
    g_in,
    bank_up,
    pu_out,
    pu_in,
    qs_out,
    qs_in,
    qy_out,
    qy_in,
    local_sem,
    send_sem,
    recv_sem,
    zf_send,
    zf_recv,
    zb_send,
    zb_recv,
):
    g, r = lax.axis_index("grp"), lax.axis_index("rep")
    y, c = g // 2, g % 2
    z, x = r // nx, r % nx
    a = y // 2
    b = ((y + 1) // 2) % 2
    share = 2 * b + c
    y_q = y + 1 - 2 * (y % 2)
    y_p = 3 - y
    half = nz // 2
    n = q_raw.shape[0]
    depth = q_raw.shape[1]
    lanes = 128
    groups = depth // lanes
    nb = nx * nz

    def at(z_, x_, y_, c_):
        return (y_ * 2 + c_, z_ * nx + x_)

    def member(m):
        cc = 1 - c if m & 1 else c
        hi = m >> 1
        yy = (y, y_q, None, y_p)[hi] if hi != 2 else 3 - y_q
        return at(z, x, yy, cc)

    loads = [
        pltpu.make_async_copy(src, dst, local_sem.at[i])
        for i, (src, dst) in enumerate(
            [(bank_in, bank_raw), (q_in, q_raw), (p_in, p_raw), (ids_in, meta_raw), (w_in, w_raw)]
        )
    ]
    for load in loads:
        load.start()

    barrier = pltpu.get_barrier_semaphore()

    def greet(device):
        pl.semaphore_signal(barrier, inc=1, device_id=device, device_id_type=MESH)

    def greet_z(i, carry):
        greet(at(lax.rem(z + i, nz), x, y, c))
        return carry

    lax.fori_loop(1, nz, greet_z, 0)
    for dx in range(1, nx):
        for yy in (y, y_p):
            greet(at(z, lax.rem(x + dx, nx), yy, c))
    for m in range(1, GROUP):
        greet(member(m))

    def remote(src, dst, send, recv, device):
        return pltpu.make_async_remote_copy(
            src_ref=src, dst_ref=dst, send_sem=send, recv_sem=recv, device_id=device, device_id_type=MESH
        )

    started = []

    def send(src, dst, index, device):
        copy = remote(src, dst, send_sem.at[index], recv_sem.at[index], device)
        copy.start()
        started.append(copy)
        return copy

    loads[0].wait()
    bank_f = bank_raw[...].astype(F32)
    for j in range(groups):
        bank_x[:, j, :] = bank_f[:, j * lanes : (j + 1) * lanes]
    bank_values = bank_x[...]
    bank_inv = 1.0 / jnp.sqrt(jnp.sum(jnp.sum(bank_values * bank_values, axis=2, keepdims=True), axis=1, keepdims=True) + EPS)
    bank_unit = bank_values * bank_inv
    bank_x[...] = bank_unit
    own_row[...] = bank_x[share].astype(BF16)

    @pl.when(a == 0)
    def _():
        gathered[0, half // 2, 0] = own_row[...]

    loads[1].wait()
    loads[3].wait()
    loads[4].wait()

    def units(raw):
        values = raw[...].astype(F32)
        inv = 1.0 / jnp.sqrt(jnp.sum(values * values, axis=1, keepdims=True) + EPS)
        return values * inv, inv

    q_unit, q_inv = units(q_raw)
    rows_q[0] = q_unit.astype(BF16)
    meta[0, 0:7, :] = meta_raw[...].astype(F32)
    meta[0, 7:8, :] = w_raw[...]
    loads[2].wait()
    p_unit, p_inv = units(p_raw)
    cols[0:n, :] = p_unit.astype(BF16)

    pl.semaphore_wait(barrier, nz - 1 + 2 * (nx - 1) + GROUP - 1)

    def z_forward(k, carry):
        offset = 2 * k + a - half

        @pl.when(offset != 0)
        def _():
            remote(
                own_row,
                gathered.at[0, k, a],
                zf_send.at[k],
                zf_recv.at[k],
                at(lax.rem(z - offset + nz, nz), x, y, c),
            ).start()

        return carry

    lax.fori_loop(0, half, z_forward, 0)

    sibling = member(1)
    neighbour = member(2)
    partner = member(6)
    to_meta = [send(meta.at[0], meta.at[m], m - 1, member(m)) for m in (1, 2, 3)]
    to_q = send(rows_q.at[0], rows_q.at[2], 3, neighbour)
    to_p = send(cols.at[pl.ds(0, n)], cols.at[pl.ds(n, n)], 4, partner)
    to_q1 = send(rows_q.at[0], rows_q.at[1], 5, sibling)

    def score(ci, s):
        logits = dot_nt(cols[ci * n : (ci + 1) * n, :], rows_q[s]) * HEAT
        e = jnp.exp(logits)
        e_t[ci * n : (ci + 1) * n, s * n : (s + 1) * n] = e
        return logits, jnp.sum(e, axis=0, keepdims=True)

    totals = [None] * 4
    logits, totals[0] = score(0, 0)
    eye = lax.broadcasted_iota(jnp.int32, (n, n), 0) == lax.broadcasted_iota(jnp.int32, (n, n), 1)
    positive = jnp.sum(jnp.where(eye, logits, 0.0), axis=0, keepdims=True)
    to_q1.wait_recv()
    totals[1] = score(0, 1)[1]
    to_q.wait_recv()
    to_q3 = send(rows_q.at[2], rows_q.at[3], 6, sibling)
    totals[2] = score(0, 2)[1]
    to_p.wait_recv()
    for s in range(3):
        totals[s] = totals[s] + score(1, s)[1]
    to_q3.wait_recv()
    totals[3] = score(0, 3)[1] + score(1, 3)[1]
    for copy in to_meta:
        copy.wait_recv()

    def z_forward_wait(k, carry):
        @pl.when(2 * k + a - half != 0)
        def _():
            remote(own_row, gathered.at[0, k, a], zf_send.at[k], zf_recv.at[k], sibling).wait_recv()

        return carry

    lax.fori_loop(0, half, z_forward_wait, 0)

    for dx in range(nx):
        for da, yy in ((0, y), (1, y_p)):
            if dx == 0 and da == 0:
                continue
            send(
                gathered.at[0, :, a],
                gathered.at[(nx - dx) % nx, :, a],
                8 + 2 * dx + da,
                at(z, lax.rem(x + dx, nx), yy, c),
            )

    row = lax.broadcasted_iota(jnp.int32, (nb, n), 0)
    row_z = lax.rem(z + lax.rem(row, nz) - half + nz, nz)
    row_x = lax.rem(x + row // nz, nx)
    row_id = (4 * (row_z * nx + row_x) + share).astype(F32)
    named = []
    for s in range(4):
        count = jnp.zeros((nb, n), F32)
        for k in range(7):
            count = count + jnp.where(row_id == meta[s, k : k + 1, :], 1.0, 0.0)
        named.append(count)

    for dx in range(nx):
        for da, aa in ((0, a), (1, 1 - a)):
            if dx or da:
                index = 8 + 2 * dx + da
                landed = gathered.at[(nx - dx) % nx, :, aa]
                remote(landed, landed, send_sem.at[index], recv_sem.at[index], sibling).wait_recv()
    wide[...] = gathered[...].reshape(nb, groups, lanes).astype(F32)
    for j in range(groups):
        cols[2 * n : 2 * n + nb, j * lanes : (j + 1) * lanes] = wide[:, j, :].astype(BF16)
    for s in range(4):
        e = jnp.exp(dot_nt(cols[2 * n : 2 * n + nb, :], rows_q[s]) * HEAT)
        e_t[2 * n : 2 * n + nb, s * n : (s + 1) * n] = e
        sums[0, s : s + 1, :] = totals[s] + jnp.sum(e * named[s], axis=0, keepdims=True)

    to_sums = [send(sums.at[0], sums.at[m], 16 + m, member(m)) for m in (1, 2, 3)]
    for copy in to_sums:
        copy.wait_recv()
    coefs, scaled, loss = [], [], None
    for s in range(4):
        total = sums[0, s : s + 1, :]
        for m in (1, 2, 3):
            total = total + sums[m, s ^ m : (s ^ m) + 1, :]
        if s == 0:
            loss = jnp.log(total) - positive
        weight = meta[s, 7:8, :] * HEAT
        scaled.append(weight)
        coefs.append(weight / total)
    loss_out[...] = loss

    for s in range(4):
        slope = (e_t[2 * n : 2 * n + nb, s * n : (s + 1) * n] * coefs[s]).astype(BF16).astype(F32)
        g_t[2 * n : 2 * n + nb, s * n : (s + 1) * n] = (slope * named[s]).astype(BF16)
    all_q = rows_q[...].reshape(4 * n, depth)
    up = dot_nn(g_t[2 * n : 2 * n + nb, :], all_q)
    for j in range(groups):
        wide[:, j, :] = up[:, j * lanes : (j + 1) * lanes]
    bank_out[...] = wide[...].astype(BF16).reshape(nx, half, 2, groups, lanes)
    to_plane_back = []
    for dx in range(nx):
        for da, (yy, aa) in ((0, (y, a)), (1, (y_p, 1 - a))):
            if dx == 0 and da == 0:
                continue
            to_plane_back.append(
                send(
                    bank_out.at[dx, :, aa],
                    plane_in.at[da, dx],
                    20 + 2 * dx + da,
                    at(z, lax.rem(x + dx, nx), yy, c),
                )
            )

    for s in range(4):
        part = (e_t[n : 2 * n, s * n : (s + 1) * n] * coefs[s]).astype(BF16)
        g_t[n : 2 * n, s * n : (s + 1) * n] = part
    pu_out[...] = dot_nn(g_t[n : 2 * n, :], all_q).astype(BF16)
    for s in range(4):
        part = e_t[0:n, s * n : (s + 1) * n] * coefs[s]
        if s == 0:
            part = part - jnp.where(eye, scaled[0], 0.0)
        g_t[0:n, s * n : (s + 1) * n] = part.astype(BF16)

    for copy in to_plane_back:
        copy.wait_recv()
    total = bank_out[0, :, a].astype(F32)
    for dx in range(nx):
        for da in range(2):
            if dx or da:
                total = total + plane_in[da, dx].astype(F32)
    z_out[...] = total.astype(BF16)

    def z_back(k, carry):
        offset = 2 * k + a - half

        @pl.when(offset != 0)
        def _():
            remote(
                z_out.at[k], z_in.at[k], zb_send.at[k], zb_recv.at[k], at(lax.rem(z + offset + nz, nz), x, y, c)
            ).start()

        return carry

    lax.fori_loop(0, half, z_back, 0)

    @pl.when(a == 0)
    def _():
        z_in[half // 2] = z_out[half // 2]

    to_pu = send(pu_out, pu_in, 28, partner)

    def query_part(s):
        return dot_tn(g_t[:, s * n : (s + 1) * n], cols[...])

    qs_out[0] = query_part(3)
    to_qs3 = send(qs_out.at[0], qs_in.at[0], 29, sibling)
    qs_out[1] = query_part(1)
    to_qs1 = send(qs_out.at[1], qs_in.at[1], 30, sibling)
    mine = query_part(2)
    to_qs3.wait_recv()
    qy_out[...] = (mine + qs_in[0]).astype(BF16)
    to_qy = send(qy_out, qy_in, 31, neighbour)
    passage_up = dot_nn(g_t[0:n, :], all_q)
    to_pu.wait_recv()
    passage_up = passage_up + pu_in[...].astype(F32)
    unit, inv = units(p_raw)
    pg_out[...] = inv * (passage_up - unit * jnp.sum(unit * passage_up, axis=1, keepdims=True))
    query_up = query_part(0)
    to_qs1.wait_recv()
    query_up = query_up + qs_in[1]
    to_qy.wait_recv()
    query_up = query_up + qy_in[...].astype(F32)
    unit, inv = units(q_raw)
    qg_out[...] = inv * (query_up - unit * jnp.sum(unit * query_up, axis=1, keepdims=True))

    def z_back_wait(k, carry):
        @pl.when(2 * k + a - half != 0)
        def _():
            remote(z_out.at[k], z_in.at[k], zb_send.at[k], zb_recv.at[k], sibling).wait_recv()

        return carry

    lax.fori_loop(0, half, z_back_wait, 0)
    g_in[0] = jnp.sum(z_in[...].astype(F32), axis=0)
    to_all = [send(g_in.at[0], g_in.at[m], 32 + m, member(m)) for m in range(1, GROUP)]
    for copy in to_all:
        copy.wait_recv()
    for delta in range(4):
        first, second = [m for m in range(GROUP) if ROW_OF[m] == delta]
        both = g_in[first] + g_in[second]
        row_b = b if delta < 2 else 1 - b
        row_c = 1 - c if delta & 1 else c
        bank_up[2 * row_b + row_c] = both
    up = bank_up[...]
    unit = bank_x[...]
    along = jnp.sum(jnp.sum(unit * up, axis=2, keepdims=True), axis=1, keepdims=True)
    bank_up[...] = bank_inv * (up - unit * along)
    for j in range(groups):
        bg_out[:, j * lanes : (j + 1) * lanes] = bank_up[:, j, :]

    for copy in started:
        copy.wait_send()

    def drain(k, carry):
        @pl.when(2 * k + a - half != 0)
        def _():
            remote(own_row, gathered.at[0, k, a], zf_send.at[k], zf_recv.at[k], sibling).wait_send()
            remote(z_out.at[k], z_in.at[k], zb_send.at[k], zb_recv.at[k], sibling).wait_send()

        return carry

    lax.fori_loop(0, half, drain, 0)


def solution(mesh):
    reps = mesh.shape["rep"]
    nx = NX
    nz = reps // nx

    def body(queries, passages, bank, hard_ids, weights):
        n, depth = queries.shape
        nb = reps
        half = nz // 2
        slab = (depth // 128, 128)
        anywhere = pl.BlockSpec(memory_space=pl.ANY)
        vmem = pl.BlockSpec(memory_space=pltpu.VMEM)
        dma = pltpu.SemaphoreType.DMA
        losses, query_grad, passage_grad, bank_grad = pl.pallas_call(
            functools.partial(kernel, nz, nx),
            out_shape=(
                jax.ShapeDtypeStruct((1, n), F32),
                jax.ShapeDtypeStruct((n, depth), F32),
                jax.ShapeDtypeStruct((n, depth), F32),
                jax.ShapeDtypeStruct((4, depth), F32),
            ),
            in_specs=[anywhere] * 5,
            out_specs=(vmem,) * 4,
            scratch_shapes=[
                pltpu.VMEM((n, depth), BF16),
                pltpu.VMEM((n, depth), BF16),
                pltpu.VMEM((4, depth), BF16),
                pltpu.VMEM((7, n), jnp.int32),
                pltpu.VMEM((1, n), F32),
                pltpu.VMEM((4, n, depth), BF16),
                pltpu.VMEM((2 * n + nb, depth), BF16),
                pltpu.VMEM((4,) + slab, F32),
                pltpu.VMEM(slab, BF16),
                pltpu.VMEM((nx, half, 2) + slab, BF16),
                pltpu.VMEM((nb,) + slab, F32),
                pltpu.VMEM((4, 8, n), F32),
                pltpu.VMEM((4, 8, n), F32),
                pltpu.VMEM((2 * n + nb, 4 * n), F32),
                pltpu.VMEM((2 * n + nb, 4 * n), BF16),
                pltpu.VMEM((nx, half, 2) + slab, BF16),
                pltpu.VMEM((2, nx, half) + slab, BF16),
                pltpu.VMEM((half,) + slab, BF16),
                pltpu.VMEM((half,) + slab, BF16),
                pltpu.VMEM((GROUP,) + slab, F32),
                pltpu.VMEM((4,) + slab, F32),
                pltpu.VMEM((n, depth), BF16),
                pltpu.VMEM((n, depth), BF16),
                pltpu.VMEM((2, n, depth), F32),
                pltpu.VMEM((2, n, depth), F32),
                pltpu.VMEM((n, depth), BF16),
                pltpu.VMEM((n, depth), BF16),
                dma((5,)),
                dma((40,)),
                dma((40,)),
                dma((half,)),
                dma((half,)),
                dma((half,)),
                dma((half,)),
            ],
            compiler_params=pltpu.CompilerParams(
                collective_id=0, has_side_effects=True, vmem_limit_bytes=40 << 20
            ),
        )(queries, passages, bank, hard_ids.T, weights.reshape(1, n))
        return losses.reshape(n), query_grad, passage_grad, bank_grad

    placed = (
        P(("grp", "rep"), None),
        P(("grp", "rep"), None),
        P("rep", None),
        P(("grp", "rep"), None),
        P(("grp", "rep")),
    )
    return jax.shard_map(
        body,
        mesh=mesh,
        in_specs=placed,
        out_specs=(
            P(("grp", "rep")),
            P(("grp", "rep"), None),
            P(("grp", "rep"), None),
            P("rep", None),
        ),
        check_vma=False,
    )
```

```python
import functools

import jax
import jax.numpy as jnp
from jax import lax
from jax.experimental import pallas as pl
from jax.experimental.pallas import tpu as pltpu
from jax.sharding import PartitionSpec as P

MESH = pl.DeviceIdType.MESH
F32 = jnp.float32
BF16 = jnp.bfloat16
EPS = 1e-06
HEAT = 20.0
NX = 4
GROUP = 8
ROW_OF = [2 * ((m >> 2 & 1) ^ (m >> 1 & 1)) + (m & 1) for m in range(GROUP)]


def dot_nt(left, right):
    return lax.dot_general(left, right, (((1,), (1,)), ((), ())), preferred_element_type=F32)


def dot_tn(left, right):
    return lax.dot_general(left, right, (((0,), (0,)), ((), ())), preferred_element_type=F32)


def dot_nn(left, right):
    return jnp.dot(left, right, preferred_element_type=F32)


def kernel(
    nz,
    nx,
    q_in,
    p_in,
    bank_in,
    ids_in,
    w_in,
    loss_out,
    qg_out,
    pg_out,
    bg_out,
    q_raw,
    p_raw,
    bank_raw,
    meta_raw,
    w_raw,
    rows_q,
    cols,
    bank_x,
    own_row,
    gathered,
    wide,
    meta,
    sums,
    e_t,
    g_t,
    bank_out,
    plane_in,
    z_out,
    z_in,
    g_in,
    bank_up,
    pu_out,
    pu_in,
    qs_out,
    qs_in,
    qy_out,
    qy_in,
    local_sem,
    send_sem,
    recv_sem,
    zf_send,
    zf_recv,
    zb_send,
    zb_recv,
):
    g, r = lax.axis_index("grp"), lax.axis_index("rep")
    y, c = g // 2, g % 2
    z, x = r // nx, r % nx
    a = y // 2
    b = ((y + 1) // 2) % 2
    share = 2 * b + c
    y_q = y + 1 - 2 * (y % 2)
    y_p = 3 - y
    half, quarter = nz // 2, nz // 4
    n = q_raw.shape[0]
    depth = q_raw.shape[1]
    lanes = 128
    groups = depth // lanes
    nb = nx * nz

    def at(z_, x_, y_, c_):
        return (y_ * 2 + c_, z_ * nx + x_)

    def member(m):
        cc = 1 - c if m & 1 else c
        hi = m >> 1
        yy = (y, y_q, None, y_p)[hi] if hi != 2 else 3 - y_q
        return at(z, x, yy, cc)

    loads = [
        pltpu.make_async_copy(src, dst, local_sem.at[i])
        for i, (src, dst) in enumerate(
            [(bank_in, bank_raw), (q_in, q_raw), (p_in, p_raw), (ids_in, meta_raw), (w_in, w_raw)]
        )
    ]
    for load in loads:
        load.start()

    barrier = pltpu.get_barrier_semaphore()

    def greet(device):
        pl.semaphore_signal(barrier, inc=1, device_id=device, device_id_type=MESH)

    def offset_of(k):
        return 2 * k + a - quarter

    def up_z(offset):
        return at(lax.rem(z + offset + nz, nz), x, y, c)

    greet(up_z(-quarter))

    @pl.when(a == 1)
    def _():
        greet(up_z(quarter))

    def greet_z(k, carry):
        @pl.when(offset_of(k) != 0)
        def _():
            greet(up_z(-offset_of(k)))

        return carry

    lax.fori_loop(0, half // 2, greet_z, 0)
    for dx in range(1, nx):
        for yy in (y, y_p):
            greet(at(z, lax.rem(x + dx, nx), yy, c))
    for m in range(1, GROUP):
        greet(member(m))

    def remote(src, dst, send, recv, device):
        return pltpu.make_async_remote_copy(
            src_ref=src, dst_ref=dst, send_sem=send, recv_sem=recv, device_id=device, device_id_type=MESH
        )

    started = []

    def send(src, dst, index, device):
        copy = remote(src, dst, send_sem.at[index], recv_sem.at[index], device)
        copy.start()
        started.append(copy)
        return copy

    loads[0].wait()
    bank_f = bank_raw[...].astype(F32)
    for j in range(groups):
        bank_x[:, j, :] = bank_f[:, j * lanes : (j + 1) * lanes]
    bank_values = bank_x[...]
    bank_inv = 1.0 / jnp.sqrt(jnp.sum(jnp.sum(bank_values * bank_values, axis=2, keepdims=True), axis=1, keepdims=True) + EPS)
    bank_unit = bank_values * bank_inv
    bank_x[...] = bank_unit
    own_row[...] = bank_x[share].astype(BF16)

    @pl.when(a == 0)
    def _():
        gathered[0, 0, nz // 8, 0] = own_row[...]

    loads[1].wait()
    loads[3].wait()
    loads[4].wait()

    def units(raw):
        values = raw[...].astype(F32)
        inv = 1.0 / jnp.sqrt(jnp.sum(values * values, axis=1, keepdims=True) + EPS)
        return values * inv, inv

    q_unit, q_inv = units(q_raw)
    rows_q[0] = q_unit.astype(BF16)
    meta[0, 0:7, :] = meta_raw[...].astype(F32)
    meta[0, 7:8, :] = w_raw[...]
    loads[2].wait()
    p_unit, p_inv = units(p_raw)
    cols[0:n, :] = p_unit.astype(BF16)

    pl.semaphore_wait(barrier, half // 2 + 2 * a + 2 * (nx - 1) + GROUP - 1)

    def z_copy(k, device):
        return remote(own_row, gathered.at[0, 0, k, a], zf_send.at[k], zf_recv.at[k], device)

    def z_forward(k, carry):
        @pl.when(offset_of(k) != 0)
        def _():
            z_copy(k, up_z(-offset_of(k))).start()

        return carry

    lax.fori_loop(0, half // 2, z_forward, 0)

    sibling = member(1)
    neighbour = member(2)
    partner = member(6)
    to_meta = [send(meta.at[0], meta.at[m], m - 1, member(m)) for m in (1, 2, 3)]
    to_q = send(rows_q.at[0], rows_q.at[2], 3, neighbour)
    to_p = send(cols.at[pl.ds(0, n)], cols.at[pl.ds(n, n)], 4, partner)
    to_q1 = send(rows_q.at[0], rows_q.at[1], 5, sibling)

    def score(ci, s):
        logits = dot_nt(cols[ci * n : (ci + 1) * n, :], rows_q[s]) * HEAT
        e = jnp.exp(logits)
        e_t[ci * n : (ci + 1) * n, s * n : (s + 1) * n] = e
        return logits, jnp.sum(e, axis=0, keepdims=True)

    def z_forward_wait(k, carry):
        @pl.when(offset_of(k) != 0)
        def _():
            z_copy(k, sibling).wait_recv()

        return carry

    def to_plane(part):
        for dx in (2, 1, 3) if nx == 4 else range(1, nx):
            for da, yy in ((0, y), (1, y_p)):
                send(
                    gathered.at[part, 0, :, a],
                    gathered.at[part, (nx - dx) % nx, :, a],
                    8 + 8 * part + 2 * dx + da,
                    at(z, lax.rem(x + dx, nx), yy, c),
                )
        send(gathered.at[part, 0, :, a], gathered.at[part, 0, :, a], 8 + 8 * part + 1, partner)

    def from_plane(part):
        for dx in range(nx):
            for da, aa in ((0, a), (1, 1 - a)):
                if dx or da:
                    index = 8 + 8 * part + 2 * dx + da
                    landed = gathered.at[part, (nx - dx) % nx, :, aa]
                    remote(landed, landed, send_sem.at[index], recv_sem.at[index], sibling).wait_recv()

    totals = [None] * 4
    logits, totals[0] = score(0, 0)
    eye = lax.broadcasted_iota(jnp.int32, (n, n), 0) == lax.broadcasted_iota(jnp.int32, (n, n), 1)
    positive = jnp.sum(jnp.where(eye, logits, 0.0), axis=0, keepdims=True)
    to_q1.wait_recv()
    totals[1] = score(0, 1)[1]
    lax.fori_loop(0, half // 2, z_forward_wait, 0)
    eighth = nz // 8
    low, high = pl.ds(0, eighth), pl.ds(eighth, eighth)
    to_high = send(gathered.at[0, 0, low, a], gathered.at[1, 0, high, a], 28, up_z(quarter))
    to_low = send(gathered.at[0, 0, high, a], gathered.at[1, 0, low, a], 29, up_z(-quarter))
    to_plane(0)

    to_q.wait_recv()
    to_q3 = send(rows_q.at[2], rows_q.at[3], 6, sibling)
    totals[2] = score(0, 2)[1]
    to_p.wait_recv()
    for s in range(3):
        totals[s] = totals[s] + score(1, s)[1]
    to_q3.wait_recv()
    totals[3] = score(0, 3)[1] + score(1, 3)[1]
    for copy in to_meta:
        copy.wait_recv()

    hb = nb // 2
    all_q = rows_q[...].reshape(4 * n, depth)

    def bank_score(part):
        first = 2 * n + part * hb
        wide[part * hb : (part + 1) * hb] = gathered[part].reshape(hb, groups, lanes).astype(F32)
        for j in range(groups):
            cols[first : first + hb, j * lanes : (j + 1) * lanes] = wide[part * hb : (part + 1) * hb, j, :].astype(BF16)
        e = jnp.exp(dot_nt(cols[first : first + hb, :], all_q) * HEAT)
        e_t[first : first + hb, :] = e
        return [jnp.sum(e[:, s * n : (s + 1) * n] * named[part][s], axis=0, keepdims=True) for s in range(4)]

    named = []
    for part in range(2):
        row = lax.broadcasted_iota(jnp.int32, (hb, n), 0)
        row_z = lax.rem(z + part * half + lax.rem(row, half) - quarter + nz, nz)
        row_x = lax.rem(x + row // half, nx)
        row_id = (4 * (row_z * nx + row_x) + share).astype(F32)
        counts = []
        for s in range(4):
            count = jnp.zeros((hb, n), F32)
            for k in range(7):
                count = count + jnp.where(row_id == meta[s, k : k + 1, :], 1.0, 0.0)
            counts.append(count)
        named.append(counts)

    from_plane(0)
    near = bank_score(0)
    to_high.wait_recv()
    to_low.wait_recv()
    to_plane(1)
    from_plane(1)
    far = bank_score(1)
    for s in range(4):
        sums[0, s : s + 1, :] = totals[s] + near[s] + far[s]

    to_sums = [send(sums.at[0], sums.at[m], 24 + m, member(m)) for m in (2, 3, 1)]
    for copy in to_sums:
        copy.wait_recv()
    coefs, scaled = [], []
    for s in range(4):
        total = sums[0, s : s + 1, :]
        for m in (1, 2, 3):
            total = total + sums[m, s ^ m : (s ^ m) + 1, :]
        if s == 0:
            loss_out[...] = jnp.log(total) - positive
        weight = meta[s, 7:8, :] * HEAT
        scaled.append(weight)
        coefs.append(weight / total)

    def bank_slopes(part):
        first, rows = 2 * n + part * hb, slice(part * hb, (part + 1) * hb)
        for s in range(4):
            slope = (e_t[first : first + hb, s * n : (s + 1) * n] * coefs[s]).astype(BF16).astype(F32)
            g_t[first : first + hb, s * n : (s + 1) * n] = (slope * named[part][s]).astype(BF16)
        up = dot_nn(g_t[first : first + hb, :], all_q)
        for j in range(groups):
            wide[rows, j, :] = up[:, j * lanes : (j + 1) * lanes]
        bank_out[part] = wide[rows].astype(BF16).reshape(nx, half // 2, 2, groups, lanes)
        copies = []
        for dx in (2, 1, 3, 0) if nx == 4 else range(nx):
            for da, (yy, aa) in ((0, (y, a)), (1, (y_p, 1 - a))):
                if dx or da:
                    copies.append(
                        send(
                            bank_out.at[part, dx, :, aa],
                            plane_in.at[part, da, dx],
                            48 + 8 * part + 2 * dx + da,
                            at(z, lax.rem(x + dx, nx), yy, c),
                        )
                    )
        return copies

    to_back = [None, bank_slopes(1)]
    to_back[0] = bank_slopes(0)

    for s in range(4):
        part = (e_t[n : 2 * n, s * n : (s + 1) * n] * coefs[s]).astype(BF16)
        g_t[n : 2 * n, s * n : (s + 1) * n] = part
    pu_out[...] = dot_nn(g_t[n : 2 * n, :], all_q).astype(BF16)
    for s in range(4):
        part = e_t[0:n, s * n : (s + 1) * n] * coefs[s]
        if s == 0:
            part = part - jnp.where(eye, scaled[0], 0.0)
        g_t[0:n, s * n : (s + 1) * n] = part.astype(BF16)

    def query_part(s):
        return dot_tn(g_t[:, s * n : (s + 1) * n], cols[...])

    qs_out[0] = query_part(3)
    to_qs3 = send(qs_out.at[0], qs_in.at[0], 37, sibling)
    qs_out[1] = query_part(1)
    to_qs1 = send(qs_out.at[1], qs_in.at[1], 38, sibling)

    def z_back_copy(k, device):
        return remote(z_out.at[k], z_in.at[k], zb_send.at[k], zb_recv.at[k], device)

    def z_back(k):
        @pl.when(offset_of(k) != 0)
        def _():
            z_back_copy(k, up_z(offset_of(k))).start()

    def z_back_far(i, carry):
        z_back(3 * nz // 8 + (1 - 2 * lax.rem(i, 2)) * ((i + 1) // 2))
        return carry

    def z_back_near(i, carry):
        z_back(i)
        return carry

    def bank_reduce(part):
        for copy in to_back[part]:
            copy.wait_recv()
        total = bank_out[part, 0, :, a].astype(F32)
        for dx in range(nx):
            for da in range(2):
                if dx or da:
                    total = total + plane_in[part, da, dx].astype(F32)
        z_out[part * (half // 2) : (part + 1) * (half // 2)] = total.astype(BF16)
        lax.fori_loop(0, half // 2, z_back_far if part else z_back_near, 0)

    bank_reduce(1)
    bank_reduce(0)

    @pl.when(a == 0)
    def _():
        z_in[nz // 8] = z_out[nz // 8]

    to_pu = send(pu_out, pu_in, 36, partner)

    mine = query_part(2)
    to_qs3.wait_recv()
    qy_out[...] = (mine + qs_in[0]).astype(BF16)
    to_qy = send(qy_out, qy_in, 39, neighbour)
    passage_up = dot_nn(g_t[0:n, :], all_q)
    to_pu.wait_recv()
    passage_up = passage_up + pu_in[...].astype(F32)
    unit, inv = units(p_raw)
    pg_out[...] = inv * (passage_up - unit * jnp.sum(unit * passage_up, axis=1, keepdims=True))
    query_up = query_part(0)
    to_qs1.wait_recv()
    query_up = query_up + qs_in[1]
    to_qy.wait_recv()
    query_up = query_up + qy_in[...].astype(F32)
    unit, inv = units(q_raw)
    qg_out[...] = inv * (query_up - unit * jnp.sum(unit * query_up, axis=1, keepdims=True))

    for copy in started:
        copy.wait_send()

    def drain(k, carry):
        @pl.when(offset_of(k) != 0)
        def _():
            z_back_copy(k, sibling).wait_send()

        return carry

    def drain_forward(k, carry):
        @pl.when(offset_of(k) != 0)
        def _():
            z_copy(k, sibling).wait_send()

        return carry

    lax.fori_loop(0, half, drain, 0)
    lax.fori_loop(0, half // 2, drain_forward, 0)

    def z_back_wait(k, carry):
        @pl.when(offset_of(k) != 0)
        def _():
            z_back_copy(k, sibling).wait_recv()

        return carry

    lax.fori_loop(0, half, z_back_wait, 0)
    g_in[0] = jnp.sum(z_in[...].astype(F32), axis=0)
    to_all = [send(g_in.at[0], g_in.at[m], 40 + m, member(m)) for m in (5, 4, 7, 6, 3, 2, 1)]
    for copy in to_all:
        copy.wait_recv()
    for delta in range(4):
        first, second = [m for m in range(GROUP) if ROW_OF[m] == delta]
        both = g_in[first] + g_in[second]
        row_b = b if delta < 2 else 1 - b
        row_c = 1 - c if delta & 1 else c
        bank_up[2 * row_b + row_c] = both
    up = bank_up[...]
    unit = bank_x[...]
    along = jnp.sum(jnp.sum(unit * up, axis=2, keepdims=True), axis=1, keepdims=True)
    bank_up[...] = bank_inv * (up - unit * along)
    for j in range(groups):
        bg_out[:, j * lanes : (j + 1) * lanes] = bank_up[:, j, :]
    for copy in to_all:
        copy.wait_send()


def hand_over(*refs):
    count = (len(refs) - 1) // 2
    sems = refs[-1]
    copies = [pltpu.make_async_copy(refs[i], refs[count + i], sems.at[i]) for i in range(count)]
    for copy in copies:
        copy.start()
    for copy in copies:
        copy.wait()


def solution(mesh):
    reps = mesh.shape["rep"]
    nx = NX
    nz = reps // nx

    def body(queries, passages, bank, hard_ids, weights):
        n, depth = queries.shape
        nb = reps
        half = nz // 2
        slab = (depth // 128, 128)
        hbm = pl.BlockSpec(memory_space=pltpu.HBM)
        vmem = pl.BlockSpec(memory_space=pltpu.VMEM)
        dma = pltpu.SemaphoreType.DMA
        results = (
            jax.ShapeDtypeStruct((1, n), F32),
            jax.ShapeDtypeStruct((n, depth), F32),
            jax.ShapeDtypeStruct((n, depth), F32),
            jax.ShapeDtypeStruct((4, depth), F32),
        )
        given = [
            pltpu.with_memory_space_constraint(value, pltpu.HBM)
            for value in (queries, passages, bank, hard_ids.T, weights.reshape(1, n))
        ]
        made = pl.pallas_call(
            functools.partial(kernel, nz, nx),
            out_shape=results,
            in_specs=[hbm] * 5,
            out_specs=(vmem,) * 4,
            scratch_shapes=[
                pltpu.VMEM((n, depth), BF16),
                pltpu.VMEM((n, depth), BF16),
                pltpu.VMEM((4, depth), BF16),
                pltpu.VMEM((7, n), jnp.int32),
                pltpu.VMEM((1, n), F32),
                pltpu.VMEM((4, n, depth), BF16),
                pltpu.VMEM((2 * n + nb, depth), BF16),
                pltpu.VMEM((4,) + slab, F32),
                pltpu.VMEM(slab, BF16),
                pltpu.VMEM((2, nx, half // 2, 2) + slab, BF16),
                pltpu.VMEM((nb,) + slab, F32),
                pltpu.VMEM((4, 8, n), F32),
                pltpu.VMEM((4, 8, n), F32),
                pltpu.VMEM((2 * n + nb, 4 * n), F32),
                pltpu.VMEM((2 * n + nb, 4 * n), BF16),
                pltpu.VMEM((2, nx, half // 2, 2) + slab, BF16),
                pltpu.VMEM((2, 2, nx, half // 2) + slab, BF16),
                pltpu.VMEM((half,) + slab, BF16),
                pltpu.VMEM((half,) + slab, BF16),
                pltpu.VMEM((GROUP,) + slab, F32),
                pltpu.VMEM((4,) + slab, F32),
                pltpu.VMEM((n, depth), BF16),
                pltpu.VMEM((n, depth), BF16),
                pltpu.VMEM((2, n, depth), F32),
                pltpu.VMEM((2, n, depth), F32),
                pltpu.VMEM((n, depth), BF16),
                pltpu.VMEM((n, depth), BF16),
                dma((5,)),
                dma((64,)),
                dma((64,)),
                dma((half // 2,)),
                dma((half // 2,)),
                dma((half,)),
                dma((half,)),
            ],
            compiler_params=pltpu.CompilerParams(
                collective_id=0, has_side_effects=True, vmem_limit_bytes=40 << 20
            ),
        )(*given)
        losses, query_grad, passage_grad, bank_grad = pl.pallas_call(
            hand_over,
            out_shape=results,
            in_specs=[vmem] * 4,
            out_specs=(hbm,) * 4,
            scratch_shapes=[dma((4,))],
        )(*made)
        return losses.reshape(n), query_grad, passage_grad, bank_grad

    placed = (
        P(("grp", "rep"), None),
        P(("grp", "rep"), None),
        P("rep", None),
        P(("grp", "rep"), None),
        P(("grp", "rep")),
    )
    return jax.shard_map(
        body,
        mesh=mesh,
        in_specs=placed,
        out_specs=(
            P(("grp", "rep")),
            P(("grp", "rep"), None),
            P(("grp", "rep"), None),
            P("rep", None),
        ),
        check_vma=False,
    )
```

```python
import functools

import jax
import jax.numpy as jnp
from jax import lax
from jax.experimental import pallas as pl
from jax.experimental.pallas import tpu as pltpu
from jax.sharding import PartitionSpec as P

MESH = pl.DeviceIdType.MESH
F32 = jnp.float32
BF16 = jnp.bfloat16
EPS = 1e-06
HEAT = 20.0
NX = 4
GROUP = 8
ROW_OF = [2 * ((m >> 2 & 1) ^ (m >> 1 & 1)) + (m & 1) for m in range(GROUP)]


def dot_nt(left, right):
    return lax.dot_general(left, right, (((1,), (1,)), ((), ())), preferred_element_type=F32)


def dot_tn(left, right):
    return lax.dot_general(left, right, (((0,), (0,)), ((), ())), preferred_element_type=F32)


def dot_nn(left, right):
    return jnp.dot(left, right, preferred_element_type=F32)


def kernel(
    nz,
    nx,
    q_in,
    p_in,
    bank_in,
    ids_in,
    w_in,
    loss_out,
    qg_out,
    pg_out,
    bg_out,
    q_raw,
    p_raw,
    bank_raw,
    meta_raw,
    w_raw,
    rows_q,
    cols,
    bank_x,
    own_row,
    gathered,
    wide,
    meta,
    sums,
    e_t,
    g_t,
    bank_out,
    plane_in,
    z_out,
    z_in,
    g_in,
    bank_up,
    pu_out,
    pu_in,
    qs_out,
    qs_in,
    qy_out,
    qy_in,
    local_sem,
    send_sem,
    recv_sem,
    zf_send,
    zf_recv,
    zb_send,
    zb_recv,
):
    g, r = lax.axis_index("grp"), lax.axis_index("rep")
    y, c = g // 2, g % 2
    z, x = r // nx, r % nx
    a = y // 2
    b = ((y + 1) // 2) % 2
    share = 2 * b + c
    y_q = y + 1 - 2 * (y % 2)
    y_p = 3 - y
    half, quarter = nz // 2, nz // 4
    n = q_raw.shape[0]
    depth = q_raw.shape[1]
    lanes = 128
    groups = depth // lanes
    nb = nx * nz

    def at(z_, x_, y_, c_):
        return (y_ * 2 + c_, z_ * nx + x_)

    def member(m):
        cc = 1 - c if m & 1 else c
        hi = m >> 1
        yy = (y, y_q, None, y_p)[hi] if hi != 2 else 3 - y_q
        return at(z, x, yy, cc)

    barrier = pltpu.get_barrier_semaphore()

    def greet(device):
        pl.semaphore_signal(barrier, inc=1, device_id=device, device_id_type=MESH)

    def offset_of(k):
        return 2 * k + a - quarter

    def up_z(offset):
        return at(lax.rem(z + offset + nz, nz), x, y, c)

    greet(up_z(-quarter))

    @pl.when(a == 1)
    def _():
        greet(up_z(quarter))

    def greet_z(k, carry):
        @pl.when(offset_of(k) != 0)
        def _():
            greet(up_z(-offset_of(k)))

        return carry

    lax.fori_loop(0, half // 2, greet_z, 0)
    for dx in range(1, nx):
        for yy in (y, y_p):
            greet(at(z, lax.rem(x + dx, nx), yy, c))
    for m in range(1, GROUP):
        greet(member(m))

    loads = [
        pltpu.make_async_copy(src, dst, local_sem.at[i])
        for i, (src, dst) in enumerate(
            [(bank_in, bank_raw), (q_in, q_raw), (p_in, p_raw), (ids_in, meta_raw), (w_in, w_raw)]
        )
    ]
    for load in loads:
        load.start()

    def remote(src, dst, send, recv, device):
        return pltpu.make_async_remote_copy(
            src_ref=src, dst_ref=dst, send_sem=send, recv_sem=recv, device_id=device, device_id_type=MESH
        )

    started = []

    def send(src, dst, index, device):
        copy = remote(src, dst, send_sem.at[index], recv_sem.at[index], device)
        copy.start()
        started.append(copy)
        return copy

    loads[0].wait()
    bank_f = bank_raw[...].astype(F32)
    for j in range(groups):
        bank_x[:, j, :] = bank_f[:, j * lanes : (j + 1) * lanes]
    bank_values = bank_x[...]
    bank_inv = 1.0 / jnp.sqrt(jnp.sum(jnp.sum(bank_values * bank_values, axis=2, keepdims=True), axis=1, keepdims=True) + EPS)
    bank_unit = bank_values * bank_inv
    bank_x[...] = bank_unit
    own_row[...] = bank_x[share].astype(BF16)

    @pl.when(a == 0)
    def _():
        gathered[0, 0, nz // 8, 0] = own_row[...]

    loads[1].wait()
    loads[3].wait()
    loads[4].wait()

    def units(raw):
        values = raw[...].astype(F32)
        inv = 1.0 / jnp.sqrt(jnp.sum(values * values, axis=1, keepdims=True) + EPS)
        return values * inv, inv

    q_unit, q_inv = units(q_raw)
    rows_q[0] = q_unit.astype(BF16)
    meta[0, 0:7, :] = meta_raw[...].astype(F32)
    meta[0, 7:8, :] = w_raw[...]
    loads[2].wait()
    p_unit, p_inv = units(p_raw)
    cols[0:n, :] = p_unit.astype(BF16)

    pl.semaphore_wait(barrier, half // 2 + 2 * a + 2 * (nx - 1) + GROUP - 1)

    def z_copy(k, device):
        return remote(own_row, gathered.at[0, 0, k, a], zf_send.at[k], zf_recv.at[k], device)

    def z_forward(k, carry):
        @pl.when(offset_of(k) != 0)
        def _():
            z_copy(k, up_z(-offset_of(k))).start()

        return carry

    lax.fori_loop(0, half // 2, z_forward, 0)

    sibling = member(1)
    neighbour = member(2)
    partner = member(6)
    to_meta = [send(meta.at[0], meta.at[m], m - 1, member(m)) for m in (1, 2, 3)]
    to_q = send(rows_q.at[0], rows_q.at[2], 3, neighbour)
    to_p = send(cols.at[pl.ds(0, n)], cols.at[pl.ds(n, n)], 4, partner)
    to_q1 = send(rows_q.at[0], rows_q.at[1], 5, sibling)

    def score(ci, s):
        logits = dot_nt(cols[ci * n : (ci + 1) * n, :], rows_q[s]) * HEAT
        e = jnp.exp(logits)
        e_t[ci * n : (ci + 1) * n, s * n : (s + 1) * n] = e
        return logits, jnp.sum(e, axis=0, keepdims=True)

    def z_forward_wait(k, carry):
        @pl.when(offset_of(k) != 0)
        def _():
            z_copy(k, sibling).wait_recv()

        return carry

    def to_plane(part):
        for dx in (2, 1, 3) if nx == 4 else range(1, nx):
            for da, yy in ((0, y), (1, y_p)):
                send(
                    gathered.at[part, 0, :, a],
                    gathered.at[part, (nx - dx) % nx, :, a],
                    8 + 8 * part + 2 * dx + da,
                    at(z, lax.rem(x + dx, nx), yy, c),
                )
        send(gathered.at[part, 0, :, a], gathered.at[part, 0, :, a], 8 + 8 * part + 1, partner)

    def from_plane(part):
        for dx in range(nx):
            for da, aa in ((0, a), (1, 1 - a)):
                if dx or da:
                    index = 8 + 8 * part + 2 * dx + da
                    landed = gathered.at[part, (nx - dx) % nx, :, aa]
                    remote(landed, landed, send_sem.at[index], recv_sem.at[index], sibling).wait_recv()

    totals = [None] * 4
    logits, totals[0] = score(0, 0)
    eye = lax.broadcasted_iota(jnp.int32, (n, n), 0) == lax.broadcasted_iota(jnp.int32, (n, n), 1)
    positive = jnp.sum(jnp.where(eye, logits, 0.0), axis=0, keepdims=True)
    to_q1.wait_recv()
    totals[1] = score(0, 1)[1]
    lax.fori_loop(0, half // 2, z_forward_wait, 0)
    eighth = nz // 8
    low, high = pl.ds(0, eighth), pl.ds(eighth, eighth)
    to_high = send(gathered.at[0, 0, low, a], gathered.at[1, 0, high, a], 28, up_z(quarter))
    to_low = send(gathered.at[0, 0, high, a], gathered.at[1, 0, low, a], 29, up_z(-quarter))
    to_plane(0)

    to_q.wait_recv()
    to_q3 = send(rows_q.at[2], rows_q.at[3], 6, sibling)
    totals[2] = score(0, 2)[1]
    to_p.wait_recv()
    for s in range(3):
        totals[s] = totals[s] + score(1, s)[1]
    to_q3.wait_recv()
    totals[3] = score(0, 3)[1] + score(1, 3)[1]
    for copy in to_meta:
        copy.wait_recv()

    hb = nb // 2
    all_q = rows_q[...].reshape(4 * n, depth)

    def bank_score(part):
        first = 2 * n + part * hb
        wide[part * hb : (part + 1) * hb] = gathered[part].reshape(hb, groups, lanes).astype(F32)
        for j in range(groups):
            cols[first : first + hb, j * lanes : (j + 1) * lanes] = wide[part * hb : (part + 1) * hb, j, :].astype(BF16)
        e = jnp.exp(dot_nt(cols[first : first + hb, :], all_q) * HEAT)
        e_t[first : first + hb, :] = e
        return [jnp.sum(e[:, s * n : (s + 1) * n] * named[part][s], axis=0, keepdims=True) for s in range(4)]

    named = []
    for part in range(2):
        row = lax.broadcasted_iota(jnp.int32, (hb, n), 0)
        row_z = lax.rem(z + part * half + lax.rem(row, half) - quarter + nz, nz)
        row_x = lax.rem(x + row // half, nx)
        row_id = (4 * (row_z * nx + row_x) + share).astype(F32)
        counts = []
        for s in range(4):
            count = jnp.zeros((hb, n), F32)
            for k in range(7):
                count = count + jnp.where(row_id == meta[s, k : k + 1, :], 1.0, 0.0)
            counts.append(count)
        named.append(counts)

    from_plane(0)
    near = bank_score(0)
    to_high.wait_recv()
    to_low.wait_recv()
    to_plane(1)
    from_plane(1)
    far = bank_score(1)
    for s in range(4):
        sums[0, s : s + 1, :] = totals[s] + near[s] + far[s]

    to_sums = [send(sums.at[0], sums.at[m], 24 + m, member(m)) for m in (2, 3, 1)]
    for copy in to_sums:
        copy.wait_recv()
    coefs, scaled = [], []
    for s in range(4):
        total = sums[0, s : s + 1, :]
        for m in (1, 2, 3):
            total = total + sums[m, s ^ m : (s ^ m) + 1, :]
        if s == 0:
            loss_out[...] = jnp.log(total) - positive
        weight = meta[s, 7:8, :] * HEAT
        scaled.append(weight)
        coefs.append(weight / total)

    def bank_slopes(part):
        first, rows = 2 * n + part * hb, slice(part * hb, (part + 1) * hb)
        for s in range(4):
            slope = (e_t[first : first + hb, s * n : (s + 1) * n] * coefs[s]).astype(BF16).astype(F32)
            g_t[first : first + hb, s * n : (s + 1) * n] = (slope * named[part][s]).astype(BF16)
        up = dot_nn(g_t[first : first + hb, :], all_q)
        for j in range(groups):
            wide[rows, j, :] = up[:, j * lanes : (j + 1) * lanes]
        bank_out[part] = wide[rows].astype(BF16).reshape(nx, half // 2, 2, groups, lanes)
        copies = []
        for dx in (2, 1, 3, 0) if nx == 4 else range(nx):
            for da, (yy, aa) in ((0, (y, a)), (1, (y_p, 1 - a))):
                if dx or da:
                    copies.append(
                        send(
                            bank_out.at[part, dx, :, aa],
                            plane_in.at[part, da, dx],
                            48 + 8 * part + 2 * dx + da,
                            at(z, lax.rem(x + dx, nx), yy, c),
                        )
                    )
        return copies

    to_back = [None, bank_slopes(1)]
    to_back[0] = bank_slopes(0)

    for s in range(4):
        part = (e_t[n : 2 * n, s * n : (s + 1) * n] * coefs[s]).astype(BF16)
        g_t[n : 2 * n, s * n : (s + 1) * n] = part
    pu_out[...] = dot_nn(g_t[n : 2 * n, :], all_q).astype(BF16)
    for s in range(4):
        part = e_t[0:n, s * n : (s + 1) * n] * coefs[s]
        if s == 0:
            part = part - jnp.where(eye, scaled[0], 0.0)
        g_t[0:n, s * n : (s + 1) * n] = part.astype(BF16)

    def query_part(s):
        return dot_tn(g_t[:, s * n : (s + 1) * n], cols[...])

    qs_out[0] = query_part(3)
    to_qs3 = send(qs_out.at[0], qs_in.at[0], 37, sibling)
    qs_out[1] = query_part(1)
    to_qs1 = send(qs_out.at[1], qs_in.at[1], 38, sibling)

    def z_back_copy(k, device):
        return remote(z_out.at[k], z_in.at[k], zb_send.at[k], zb_recv.at[k], device)

    def z_back(k):
        @pl.when(offset_of(k) != 0)
        def _():
            z_back_copy(k, up_z(offset_of(k))).start()

    def z_back_far(i, carry):
        z_back(3 * nz // 8 + (1 - 2 * lax.rem(i, 2)) * ((i + 1) // 2))
        return carry

    def z_back_near(i, carry):
        z_back(i)
        return carry

    def bank_reduce(part):
        for copy in to_back[part]:
            copy.wait_recv()
        total = bank_out[part, 0, :, a].astype(F32)
        for dx in range(nx):
            for da in range(2):
                if dx or da:
                    total = total + plane_in[part, da, dx].astype(F32)
        z_out[part * (half // 2) : (part + 1) * (half // 2)] = total.astype(BF16)
        lax.fori_loop(0, half // 2, z_back_far if part else z_back_near, 0)

    bank_reduce(1)
    bank_reduce(0)

    @pl.when(a == 0)
    def _():
        z_in[nz // 8] = z_out[nz // 8]

    to_pu = send(pu_out, pu_in, 36, partner)

    mine = query_part(2)
    to_qs3.wait_recv()
    qy_out[...] = (mine + qs_in[0]).astype(BF16)
    to_qy = send(qy_out, qy_in, 39, neighbour)
    passage_up = dot_nn(g_t[0:n, :], all_q)
    to_pu.wait_recv()
    passage_up = passage_up + pu_in[...].astype(F32)
    unit, inv = units(p_raw)
    pg_out[...] = inv * (passage_up - unit * jnp.sum(unit * passage_up, axis=1, keepdims=True))
    query_up = query_part(0)
    to_qs1.wait_recv()
    query_up = query_up + qs_in[1]
    to_qy.wait_recv()
    query_up = query_up + qy_in[...].astype(F32)
    unit, inv = units(q_raw)
    qg_out[...] = inv * (query_up - unit * jnp.sum(unit * query_up, axis=1, keepdims=True))

    for copy in started:
        copy.wait_send()

    def drain(k, carry):
        @pl.when(offset_of(k) != 0)
        def _():
            z_back_copy(k, sibling).wait_send()

        return carry

    def drain_forward(k, carry):
        @pl.when(offset_of(k) != 0)
        def _():
            z_copy(k, sibling).wait_send()

        return carry

    lax.fori_loop(0, half, drain, 0)
    lax.fori_loop(0, half // 2, drain_forward, 0)

    def z_back_wait(k, carry):
        @pl.when(offset_of(k) != 0)
        def _():
            z_back_copy(k, sibling).wait_recv()

        return carry

    lax.fori_loop(0, half, z_back_wait, 0)
    g_in[0] = jnp.sum(z_in[...].astype(F32), axis=0)
    to_all = [send(g_in.at[0], g_in.at[m], 40 + m, member(m)) for m in (5, 4, 7, 6, 3, 2, 1)]
    for copy in to_all:
        copy.wait_recv()
    for delta in range(4):
        first, second = [m for m in range(GROUP) if ROW_OF[m] == delta]
        both = g_in[first] + g_in[second]
        row_b = b if delta < 2 else 1 - b
        row_c = 1 - c if delta & 1 else c
        bank_up[2 * row_b + row_c] = both
    up = bank_up[...]
    unit = bank_x[...]
    along = jnp.sum(jnp.sum(unit * up, axis=2, keepdims=True), axis=1, keepdims=True)
    bank_up[...] = bank_inv * (up - unit * along)
    for j in range(groups):
        bg_out[:, j * lanes : (j + 1) * lanes] = bank_up[:, j, :]
    for copy in to_all:
        copy.wait_send()


def hand_over(*refs):
    count = (len(refs) - 1) // 2
    sems = refs[-1]
    copies = [pltpu.make_async_copy(refs[i], refs[count + i], sems.at[i]) for i in range(count)]
    for copy in copies:
        copy.start()
    for copy in copies:
        copy.wait()


def solution(mesh):
    reps = mesh.shape["rep"]
    nx = NX
    nz = reps // nx

    def body(queries, passages, bank, hard_ids, weights):
        n, depth = queries.shape
        nb = reps
        half = nz // 2
        slab = (depth // 128, 128)
        hbm = pl.BlockSpec(memory_space=pltpu.HBM)
        vmem = pl.BlockSpec(memory_space=pltpu.VMEM)
        dma = pltpu.SemaphoreType.DMA
        results = (
            jax.ShapeDtypeStruct((1, n), F32),
            jax.ShapeDtypeStruct((n, depth), F32),
            jax.ShapeDtypeStruct((n, depth), F32),
            jax.ShapeDtypeStruct((4, depth), F32),
        )
        given = [
            pltpu.with_memory_space_constraint(value, pltpu.HBM)
            for value in (queries, passages, bank, hard_ids.T, weights.reshape(1, n))
        ]
        made = pl.pallas_call(
            functools.partial(kernel, nz, nx),
            out_shape=results,
            in_specs=[hbm] * 5,
            out_specs=(vmem,) * 4,
            scratch_shapes=[
                pltpu.VMEM((n, depth), BF16),
                pltpu.VMEM((n, depth), BF16),
                pltpu.VMEM((4, depth), BF16),
                pltpu.VMEM((7, n), jnp.int32),
                pltpu.VMEM((1, n), F32),
                pltpu.VMEM((4, n, depth), BF16),
                pltpu.VMEM((2 * n + nb, depth), BF16),
                pltpu.VMEM((4,) + slab, F32),
                pltpu.VMEM(slab, BF16),
                pltpu.VMEM((2, nx, half // 2, 2) + slab, BF16),
                pltpu.VMEM((nb,) + slab, F32),
                pltpu.VMEM((4, 8, n), F32),
                pltpu.VMEM((4, 8, n), F32),
                pltpu.VMEM((2 * n + nb, 4 * n), F32),
                pltpu.VMEM((2 * n + nb, 4 * n), BF16),
                pltpu.VMEM((2, nx, half // 2, 2) + slab, BF16),
                pltpu.VMEM((2, 2, nx, half // 2) + slab, BF16),
                pltpu.VMEM((half,) + slab, BF16),
                pltpu.VMEM((half,) + slab, BF16),
                pltpu.VMEM((GROUP,) + slab, F32),
                pltpu.VMEM((4,) + slab, F32),
                pltpu.VMEM((n, depth), BF16),
                pltpu.VMEM((n, depth), BF16),
                pltpu.VMEM((2, n, depth), F32),
                pltpu.VMEM((2, n, depth), F32),
                pltpu.VMEM((n, depth), BF16),
                pltpu.VMEM((n, depth), BF16),
                dma((5,)),
                dma((64,)),
                dma((64,)),
                dma((half // 2,)),
                dma((half // 2,)),
                dma((half,)),
                dma((half,)),
            ],
            compiler_params=pltpu.CompilerParams(
                collective_id=0, has_side_effects=True, vmem_limit_bytes=40 << 20
            ),
        )(*given)
        losses, query_grad, passage_grad, bank_grad = pl.pallas_call(
            hand_over,
            out_shape=results,
            in_specs=[vmem] * 4,
            out_specs=(hbm,) * 4,
            scratch_shapes=[dma((4,))],
            compiler_params=pltpu.CompilerParams(vmem_limit_bytes=1 << 20),
        )(*made)
        return losses.reshape(n), query_grad, passage_grad, bank_grad

    placed = (
        P(("grp", "rep"), None),
        P(("grp", "rep"), None),
        P("rep", None),
        P(("grp", "rep"), None),
        P(("grp", "rep")),
    )
    return jax.shard_map(
        body,
        mesh=mesh,
        in_specs=placed,
        out_specs=(
            P(("grp", "rep")),
            P(("grp", "rep"), None),
            P(("grp", "rep"), None),
            P("rep", None),
        ),
        check_vma=False,
    )
```

```python
import functools

import jax
import jax.numpy as jnp
from jax import lax
from jax.experimental import pallas as pl
from jax.experimental.pallas import tpu as pltpu
from jax.sharding import PartitionSpec as P

MESH = pl.DeviceIdType.MESH
F32 = jnp.float32
BF16 = jnp.bfloat16
EPS = 1e-06
HEAT = 20.0
NX = 4
GROUP = 8
ROW_OF = [2 * ((m >> 2 & 1) ^ (m >> 1 & 1)) + (m & 1) for m in range(GROUP)]


def dot_nt(left, right):
    return lax.dot_general(left, right, (((1,), (1,)), ((), ())), preferred_element_type=F32)


def dot_tn(left, right):
    return lax.dot_general(left, right, (((0,), (0,)), ((), ())), preferred_element_type=F32)


def dot_nn(left, right):
    return jnp.dot(left, right, preferred_element_type=F32)


def kernel(
    nz,
    nx,
    q_in,
    p_in,
    bank_in,
    ids_in,
    w_in,
    loss_out,
    qg_out,
    pg_out,
    up_out,
    unit_out,
    inv_out,
    q_raw,
    p_raw,
    bank_raw,
    meta_raw,
    w_raw,
    rows_q,
    cols,
    bank_x,
    own_row,
    gathered,
    wide,
    meta,
    sums,
    e_t,
    g_t,
    bank_out,
    plane_in,
    z_out,
    z_in,
    g_in,
    pu_out,
    pu_in,
    qs_out,
    qs_in,
    qy_out,
    qy_in,
    local_sem,
    send_sem,
    recv_sem,
    zf_send,
    zf_recv,
    zb_send,
    zb_recv,
):
    g, r = lax.axis_index("grp"), lax.axis_index("rep")
    y, c = g // 2, g % 2
    z, x = r // nx, r % nx
    a = y // 2
    b = ((y + 1) // 2) % 2
    share = 2 * b + c
    y_q = y + 1 - 2 * (y % 2)
    y_p = 3 - y
    half, quarter = nz // 2, nz // 4
    n = q_raw.shape[0]
    depth = q_raw.shape[1]
    lanes = 128
    groups = depth // lanes
    nb = nx * nz

    def at(z_, x_, y_, c_):
        return (y_ * 2 + c_, z_ * nx + x_)

    def member(m):
        cc = 1 - c if m & 1 else c
        hi = m >> 1
        yy = (y, y_q, None, y_p)[hi] if hi != 2 else 3 - y_q
        return at(z, x, yy, cc)

    barrier = pltpu.get_barrier_semaphore()

    def greet(device):
        pl.semaphore_signal(barrier, inc=1, device_id=device, device_id_type=MESH)

    def offset_of(k):
        return 2 * k + a - quarter

    def up_z(offset):
        return at(lax.rem(z + offset + nz, nz), x, y, c)

    greet(up_z(-quarter))

    @pl.when(a == 1)
    def _():
        greet(up_z(quarter))

    def greet_z(k, carry):
        @pl.when(offset_of(k) != 0)
        def _():
            greet(up_z(-offset_of(k)))

        return carry

    lax.fori_loop(0, half // 2, greet_z, 0)
    for dx in range(1, nx):
        for yy in (y, y_p):
            greet(at(z, lax.rem(x + dx, nx), yy, c))
    for m in range(1, GROUP):
        greet(member(m))

    loads = [
        pltpu.make_async_copy(src, dst, local_sem.at[i])
        for i, (src, dst) in enumerate(
            [(bank_in, bank_raw), (q_in, q_raw), (p_in, p_raw), (ids_in, meta_raw), (w_in, w_raw)]
        )
    ]
    for load in loads:
        load.start()

    def remote(src, dst, send, recv, device):
        return pltpu.make_async_remote_copy(
            src_ref=src, dst_ref=dst, send_sem=send, recv_sem=recv, device_id=device, device_id_type=MESH
        )

    started = []

    def send(src, dst, index, device):
        copy = remote(src, dst, send_sem.at[index], recv_sem.at[index], device)
        copy.start()
        started.append(copy)
        return copy

    loads[0].wait()
    bank_f = bank_raw[...].astype(F32)
    for j in range(groups):
        bank_x[:, j, :] = bank_f[:, j * lanes : (j + 1) * lanes]
    bank_values = bank_x[...]
    bank_inv = 1.0 / jnp.sqrt(jnp.sum(jnp.sum(bank_values * bank_values, axis=2, keepdims=True), axis=1, keepdims=True) + EPS)
    bank_unit = bank_values * bank_inv
    bank_x[...] = bank_unit
    own_row[...] = bank_x[share].astype(BF16)

    @pl.when(a == 0)
    def _():
        gathered[0, 0, nz // 8, 0] = own_row[...]

    loads[1].wait()
    loads[3].wait()
    loads[4].wait()

    def units(raw):
        values = raw[...].astype(F32)
        inv = 1.0 / jnp.sqrt(jnp.sum(values * values, axis=1, keepdims=True) + EPS)
        return values * inv, inv

    q_unit, q_inv = units(q_raw)
    rows_q[0] = q_unit.astype(BF16)
    meta[0, 0:7, :] = meta_raw[...].astype(F32)
    meta[0, 7:8, :] = w_raw[...]
    loads[2].wait()
    p_unit, p_inv = units(p_raw)
    cols[0:n, :] = p_unit.astype(BF16)

    pl.semaphore_wait(barrier, half // 2 + 2 * a + 2 * (nx - 1) + GROUP - 1)

    def z_copy(k, device):
        return remote(own_row, gathered.at[0, 0, k, a], zf_send.at[k], zf_recv.at[k], device)

    def z_forward(k, carry):
        @pl.when(offset_of(k) != 0)
        def _():
            z_copy(k, up_z(-offset_of(k))).start()

        return carry

    lax.fori_loop(0, half // 2, z_forward, 0)

    sibling = member(1)
    neighbour = member(2)
    partner = member(6)
    to_meta = [send(meta.at[0], meta.at[m], m - 1, member(m)) for m in (1, 2, 3)]
    to_q = send(rows_q.at[0], rows_q.at[2], 3, neighbour)
    to_p = send(cols.at[pl.ds(0, n)], cols.at[pl.ds(n, n)], 4, partner)
    to_q1 = send(rows_q.at[0], rows_q.at[1], 5, sibling)

    def score(ci, s):
        logits = dot_nt(cols[ci * n : (ci + 1) * n, :], rows_q[s]) * HEAT
        e = jnp.exp(logits)
        e_t[ci * n : (ci + 1) * n, s * n : (s + 1) * n] = e
        return logits, jnp.sum(e, axis=0, keepdims=True)

    def z_forward_wait(k, carry):
        @pl.when(offset_of(k) != 0)
        def _():
            z_copy(k, sibling).wait_recv()

        return carry

    def to_plane(part):
        for dx in (2, 1, 3) if nx == 4 else range(1, nx):
            for da, yy in ((0, y), (1, y_p)):
                send(
                    gathered.at[part, 0, :, a],
                    gathered.at[part, (nx - dx) % nx, :, a],
                    8 + 8 * part + 2 * dx + da,
                    at(z, lax.rem(x + dx, nx), yy, c),
                )
        send(gathered.at[part, 0, :, a], gathered.at[part, 0, :, a], 8 + 8 * part + 1, partner)

    def from_plane(part):
        for dx in range(nx):
            for da, aa in ((0, a), (1, 1 - a)):
                if dx or da:
                    index = 8 + 8 * part + 2 * dx + da
                    landed = gathered.at[part, (nx - dx) % nx, :, aa]
                    remote(landed, landed, send_sem.at[index], recv_sem.at[index], sibling).wait_recv()

    totals = [None] * 4
    logits, totals[0] = score(0, 0)
    eye = lax.broadcasted_iota(jnp.int32, (n, n), 0) == lax.broadcasted_iota(jnp.int32, (n, n), 1)
    positive = jnp.sum(jnp.where(eye, logits, 0.0), axis=0, keepdims=True)
    to_q1.wait_recv()
    totals[1] = score(0, 1)[1]
    lax.fori_loop(0, half // 2, z_forward_wait, 0)
    eighth = nz // 8
    low, high = pl.ds(0, eighth), pl.ds(eighth, eighth)
    to_high = send(gathered.at[0, 0, low, a], gathered.at[1, 0, high, a], 28, up_z(quarter))
    to_low = send(gathered.at[0, 0, high, a], gathered.at[1, 0, low, a], 29, up_z(-quarter))
    to_plane(0)

    to_q.wait_recv()
    to_q3 = send(rows_q.at[2], rows_q.at[3], 6, sibling)
    totals[2] = score(0, 2)[1]
    to_p.wait_recv()
    for s in range(3):
        totals[s] = totals[s] + score(1, s)[1]
    to_q3.wait_recv()
    totals[3] = score(0, 3)[1] + score(1, 3)[1]
    for copy in to_meta:
        copy.wait_recv()

    hb = nb // 2
    all_q = rows_q[...].reshape(4 * n, depth)

    def bank_score(part):
        first = 2 * n + part * hb
        wide[part * hb : (part + 1) * hb] = gathered[part].reshape(hb, groups, lanes).astype(F32)
        for j in range(groups):
            cols[first : first + hb, j * lanes : (j + 1) * lanes] = wide[part * hb : (part + 1) * hb, j, :].astype(BF16)
        e = jnp.exp(dot_nt(cols[first : first + hb, :], all_q) * HEAT)
        e_t[first : first + hb, :] = e
        return [jnp.sum(e[:, s * n : (s + 1) * n] * named[part][s], axis=0, keepdims=True) for s in range(4)]

    named = []
    for part in range(2):
        row = lax.broadcasted_iota(jnp.int32, (hb, n), 0)
        row_z = lax.rem(z + part * half + lax.rem(row, half) - quarter + nz, nz)
        row_x = lax.rem(x + row // half, nx)
        row_id = (4 * (row_z * nx + row_x) + share).astype(F32)
        counts = []
        for s in range(4):
            count = jnp.zeros((hb, n), F32)
            for k in range(7):
                count = count + jnp.where(row_id == meta[s, k : k + 1, :], 1.0, 0.0)
            counts.append(count)
        named.append(counts)

    from_plane(0)
    near = bank_score(0)
    to_high.wait_recv()
    to_low.wait_recv()
    to_plane(1)
    from_plane(1)
    far = bank_score(1)
    for s in range(4):
        sums[0, s : s + 1, :] = totals[s] + near[s] + far[s]

    to_sums = [send(sums.at[0], sums.at[m], 24 + m, member(m)) for m in (2, 3, 1)]
    for copy in to_sums:
        copy.wait_recv()
    coefs, scaled = [], []
    for s in range(4):
        total = sums[0, s : s + 1, :]
        for m in (1, 2, 3):
            total = total + sums[m, s ^ m : (s ^ m) + 1, :]
        if s == 0:
            own_total = total
        weight = meta[s, 7:8, :] * HEAT
        scaled.append(weight)
        coefs.append(weight / total)

    def bank_slopes(part):
        first, rows = 2 * n + part * hb, slice(part * hb, (part + 1) * hb)
        for s in range(4):
            slope = (e_t[first : first + hb, s * n : (s + 1) * n] * coefs[s]).astype(BF16).astype(F32)
            g_t[first : first + hb, s * n : (s + 1) * n] = (slope * named[part][s]).astype(BF16)
        up = dot_nn(g_t[first : first + hb, :], all_q)
        for j in range(groups):
            wide[rows, j, :] = up[:, j * lanes : (j + 1) * lanes]
        bank_out[part] = wide[rows].astype(BF16).reshape(nx, half // 2, 2, groups, lanes)
        copies = []
        for dx in (2, 1, 3, 0) if nx == 4 else range(nx):
            for da, (yy, aa) in ((0, (y, a)), (1, (y_p, 1 - a))):
                if dx or da:
                    copies.append(
                        send(
                            bank_out.at[part, dx, :, aa],
                            plane_in.at[part, da, dx],
                            48 + 8 * part + 2 * dx + da,
                            at(z, lax.rem(x + dx, nx), yy, c),
                        )
                    )
        return copies

    to_back = [None, bank_slopes(1)]
    to_back[0] = bank_slopes(0)

    loss_out[...] = jnp.log(own_total) - positive

    for s in range(4):
        part = (e_t[n : 2 * n, s * n : (s + 1) * n] * coefs[s]).astype(BF16)
        g_t[n : 2 * n, s * n : (s + 1) * n] = part
    pu_out[...] = dot_nn(g_t[n : 2 * n, :], all_q).astype(BF16)
    for s in range(4):
        part = e_t[0:n, s * n : (s + 1) * n] * coefs[s]
        if s == 0:
            part = part - jnp.where(eye, scaled[0], 0.0)
        g_t[0:n, s * n : (s + 1) * n] = part.astype(BF16)

    def query_part(s):
        return dot_tn(g_t[:, s * n : (s + 1) * n], cols[...])

    qs_out[0] = query_part(3)
    to_qs3 = send(qs_out.at[0], qs_in.at[0], 37, sibling)
    qs_out[1] = query_part(1)
    to_qs1 = send(qs_out.at[1], qs_in.at[1], 38, sibling)

    def z_back_copy(k, device):
        return remote(z_out.at[k], z_in.at[k], zb_send.at[k], zb_recv.at[k], device)

    def z_back_near(k, carry):
        @pl.when(offset_of(k) != 0)
        def _():
            z_back_copy(k, up_z(offset_of(k))).start()

        return carry

    def bank_reduce(part):
        for copy in to_back[part]:
            copy.wait_recv()
        total = bank_out[part, 0, :, a].astype(F32)
        for dx in range(nx):
            for da in range(2):
                if dx or da:
                    total = total + plane_in[part, da, dx].astype(F32)
        z_out[part * (half // 2) : (part + 1) * (half // 2)] = total.astype(BF16)
        if part:
            for i in range(half // 2):
                k = 3 * nz // 8 + (1 - 2 * (i % 2)) * ((i + 1) // 2)
                z_back_copy(k, up_z(offset_of(k))).start()
        else:
            lax.fori_loop(0, half // 2, z_back_near, 0)

    bank_reduce(1)
    bank_reduce(0)

    @pl.when(a == 0)
    def _():
        z_in[nz // 8] = z_out[nz // 8]

    to_pu = send(pu_out, pu_in, 36, partner)

    mine = query_part(2)
    to_qs3.wait_recv()
    qy_out[...] = (mine + qs_in[0]).astype(BF16)
    to_qy = send(qy_out, qy_in, 39, neighbour)
    passage_up = dot_nn(g_t[0:n, :], all_q)
    to_pu.wait_recv()
    passage_up = passage_up + pu_in[...].astype(F32)
    unit, inv = units(p_raw)
    pg_out[...] = inv * (passage_up - unit * jnp.sum(unit * passage_up, axis=1, keepdims=True))
    query_up = query_part(0)
    to_qs1.wait_recv()
    query_up = query_up + qs_in[1]
    to_qy.wait_recv()
    query_up = query_up + qy_in[...].astype(F32)
    unit, inv = units(q_raw)
    qg_out[...] = inv * (query_up - unit * jnp.sum(unit * query_up, axis=1, keepdims=True))

    unit_out[...] = bank_x[...]
    inv_out[...] = jnp.broadcast_to(bank_inv, inv_out.shape)

    for copy in started:
        copy.wait_send()

    def drain(k, carry):
        @pl.when(offset_of(k) != 0)
        def _():
            z_back_copy(k, sibling).wait_send()

        return carry

    def drain_forward(k, carry):
        @pl.when(offset_of(k) != 0)
        def _():
            z_copy(k, sibling).wait_send()

        return carry

    lax.fori_loop(0, half, drain, 0)
    lax.fori_loop(0, half // 2, drain_forward, 0)

    def z_back_wait(k, carry):
        @pl.when(offset_of(k) != 0)
        def _():
            z_back_copy(k, sibling).wait_recv()

        return carry

    lax.fori_loop(0, half, z_back_wait, 0)
    g_in[0] = jnp.sum(z_in[...].astype(F32), axis=0)
    to_all = [send(g_in.at[0], g_in.at[m], 40 + m, member(m)) for m in (5, 4, 7, 6, 3, 2, 1)]
    for copy in to_all:
        copy.wait_recv()
    for delta in range(4):
        first, second = [m for m in range(GROUP) if ROW_OF[m] == delta]
        both = g_in[first] + g_in[second]
        row_b = b if delta < 2 else 1 - b
        row_c = 1 - c if delta & 1 else c
        up_out[2 * row_b + row_c] = both
    for copy in to_all:
        copy.wait_send()


def finish(loss, qg, pg, up_ref, unit_ref, inv_ref, loss_out, qg_out, pg_out, bg_out, slabs, rows, sems):
    copies = [pltpu.make_async_copy(loss, loss_out, sems.at[0])]
    copies += [pltpu.make_async_copy(qg, qg_out, sems.at[1]), pltpu.make_async_copy(pg, pg_out, sems.at[2])]
    for copy in copies:
        copy.start()
    up, unit = up_ref[...], unit_ref[...]
    along = jnp.sum(jnp.sum(unit * up, axis=2, keepdims=True), axis=1, keepdims=True)
    slabs[...] = inv_ref[...] * (up - unit * along)
    for j in range(slabs.shape[1]):
        rows[:, j * 128 : (j + 1) * 128] = slabs[:, j, :]
    last = pltpu.make_async_copy(rows, bg_out, sems.at[3])
    last.start()
    for copy in copies:
        copy.wait()
    last.wait()


def solution(mesh):
    reps = mesh.shape["rep"]
    nx = NX
    nz = reps // nx

    def body(queries, passages, bank, hard_ids, weights):
        n, depth = queries.shape
        nb = reps
        half = nz // 2
        slab = (depth // 128, 128)
        hbm = pl.BlockSpec(memory_space=pltpu.HBM)
        vmem = pl.BlockSpec(memory_space=pltpu.VMEM)
        dma = pltpu.SemaphoreType.DMA
        results = (
            jax.ShapeDtypeStruct((1, n), F32),
            jax.ShapeDtypeStruct((n, depth), F32),
            jax.ShapeDtypeStruct((n, depth), F32),
        )
        small = jax.ShapeDtypeStruct((4,) + slab, F32)
        given = [
            pltpu.with_memory_space_constraint(value, pltpu.HBM)
            for value in (queries, passages, bank, hard_ids.T, weights.reshape(1, n))
        ]
        made = pl.pallas_call(
            functools.partial(kernel, nz, nx),
            out_shape=results + (small,) * 3,
            in_specs=[hbm] * 5,
            out_specs=(vmem,) * 6,
            scratch_shapes=[
                pltpu.VMEM((n, depth), BF16),
                pltpu.VMEM((n, depth), BF16),
                pltpu.VMEM((4, depth), BF16),
                pltpu.VMEM((7, n), jnp.int32),
                pltpu.VMEM((1, n), F32),
                pltpu.VMEM((4, n, depth), BF16),
                pltpu.VMEM((2 * n + nb, depth), BF16),
                pltpu.VMEM((4,) + slab, F32),
                pltpu.VMEM(slab, BF16),
                pltpu.VMEM((2, nx, half // 2, 2) + slab, BF16),
                pltpu.VMEM((nb,) + slab, F32),
                pltpu.VMEM((4, 8, n), F32),
                pltpu.VMEM((4, 8, n), F32),
                pltpu.VMEM((2 * n + nb, 4 * n), F32),
                pltpu.VMEM((2 * n + nb, 4 * n), BF16),
                pltpu.VMEM((2, nx, half // 2, 2) + slab, BF16),
                pltpu.VMEM((2, 2, nx, half // 2) + slab, BF16),
                pltpu.VMEM((half,) + slab, BF16),
                pltpu.VMEM((half,) + slab, BF16),
                pltpu.VMEM((GROUP,) + slab, F32),
                pltpu.VMEM((n, depth), BF16),
                pltpu.VMEM((n, depth), BF16),
                pltpu.VMEM((2, n, depth), F32),
                pltpu.VMEM((2, n, depth), F32),
                pltpu.VMEM((n, depth), BF16),
                pltpu.VMEM((n, depth), BF16),
                dma((5,)),
                dma((64,)),
                dma((64,)),
                dma((half // 2,)),
                dma((half // 2,)),
                dma((half,)),
                dma((half,)),
            ],
            compiler_params=pltpu.CompilerParams(
                collective_id=0, has_side_effects=True, vmem_limit_bytes=40 << 20
            ),
        )(*given)
        losses, query_grad, passage_grad, bank_grad = pl.pallas_call(
            finish,
            out_shape=results + (jax.ShapeDtypeStruct((4, depth), F32),),
            in_specs=[vmem] * 6,
            out_specs=(hbm,) * 4,
            scratch_shapes=[pltpu.VMEM((4,) + slab, F32), pltpu.VMEM((4, depth), F32), dma((4,))],
            compiler_params=pltpu.CompilerParams(vmem_limit_bytes=1 << 20),
        )(*made)
        return losses.reshape(n), query_grad, passage_grad, bank_grad

    placed = (
        P(("grp", "rep"), None),
        P(("grp", "rep"), None),
        P("rep", None),
        P(("grp", "rep"), None),
        P(("grp", "rep")),
    )
    return jax.shard_map(
        body,
        mesh=mesh,
        in_specs=placed,
        out_specs=(
            P(("grp", "rep")),
            P(("grp", "rep"), None),
            P(("grp", "rep"), None),
            P("rep", None),
        ),
        check_vma=False,
    )
```

```python
import functools

import jax
import jax.numpy as jnp
from jax import lax
from jax.experimental import pallas as pl
from jax.experimental.pallas import tpu as pltpu
from jax.sharding import PartitionSpec as P

MESH = pl.DeviceIdType.MESH
F32 = jnp.float32
BF16 = jnp.bfloat16
EPS = 1e-06
HEAT = 20.0
NX = 4
GROUP = 8
ROW_OF = [2 * ((m >> 2 & 1) ^ (m >> 1 & 1)) + (m & 1) for m in range(GROUP)]


def dot_nt(left, right):
    return lax.dot_general(left, right, (((1,), (1,)), ((), ())), preferred_element_type=F32)


def dot_tn(left, right):
    return lax.dot_general(left, right, (((0,), (0,)), ((), ())), preferred_element_type=F32)


def dot_nn(left, right):
    return jnp.dot(left, right, preferred_element_type=F32)


def kernel(
    nz,
    nx,
    q_in,
    p_in,
    bank_in,
    ids_in,
    w_in,
    loss_out,
    qg_out,
    pg_out,
    up_out,
    unit_out,
    inv_out,
    q_raw,
    p_raw,
    bank_raw,
    meta_raw,
    w_raw,
    rows_q,
    cols,
    bank_x,
    own_row,
    gathered,
    wide,
    meta,
    sums,
    e_t,
    g_t,
    bank_out,
    plane_in,
    z_out,
    z_in,
    g_in,
    pu_out,
    pu_in,
    qs_out,
    qs_in,
    qy_out,
    qy_in,
    local_sem,
    send_sem,
    recv_sem,
    zf_send,
    zf_recv,
    zb_send,
    zb_recv,
):
    g, r = lax.axis_index("grp"), lax.axis_index("rep")
    y, c = g // 2, g % 2
    z, x = r // nx, r % nx
    a = y // 2
    b = ((y + 1) // 2) % 2
    share = 2 * b + c
    y_q = y + 1 - 2 * (y % 2)
    y_p = 3 - y
    half, quarter = nz // 2, nz // 4
    n = q_raw.shape[0]
    depth = q_raw.shape[1]
    lanes = 128
    groups = depth // lanes
    nb = nx * nz

    def at(z_, x_, y_, c_):
        return (y_ * 2 + c_, z_ * nx + x_)

    def member(m):
        cc = 1 - c if m & 1 else c
        hi = m >> 1
        yy = (y, y_q, None, y_p)[hi] if hi != 2 else 3 - y_q
        return at(z, x, yy, cc)

    barrier = pltpu.get_barrier_semaphore()

    def greet(device):
        pl.semaphore_signal(barrier, inc=1, device_id=device, device_id_type=MESH)

    def offset_of(k):
        return 2 * k + a - quarter

    def up_z(offset):
        return at(lax.rem(z + offset + nz, nz), x, y, c)

    greet(up_z(-quarter))

    @pl.when(a == 1)
    def _():
        greet(up_z(quarter))

    def greet_z(k, carry):
        @pl.when(offset_of(k) != 0)
        def _():
            greet(up_z(-offset_of(k)))

        return carry

    lax.fori_loop(0, half // 2, greet_z, 0)
    for dx in range(1, nx):
        for yy in (y, y_p):
            greet(at(z, lax.rem(x + dx, nx), yy, c))
    for m in range(1, GROUP):
        greet(member(m))

    loads = [
        pltpu.make_async_copy(src, dst, local_sem.at[i])
        for i, (src, dst) in enumerate(
            [(bank_in, bank_raw), (q_in, q_raw), (p_in, p_raw), (ids_in, meta_raw), (w_in, w_raw)]
        )
    ]
    for load in loads:
        load.start()

    def remote(src, dst, send, recv, device):
        return pltpu.make_async_remote_copy(
            src_ref=src, dst_ref=dst, send_sem=send, recv_sem=recv, device_id=device, device_id_type=MESH
        )

    started = []

    def send(src, dst, index, device):
        copy = remote(src, dst, send_sem.at[index], recv_sem.at[index], device)
        copy.start()
        started.append(copy)
        return copy

    loads[0].wait()
    bank_f = bank_raw[...].astype(F32)
    for j in range(groups):
        bank_x[:, j, :] = bank_f[:, j * lanes : (j + 1) * lanes]
    bank_values = bank_x[...]
    bank_inv = 1.0 / jnp.sqrt(jnp.sum(jnp.sum(bank_values * bank_values, axis=2, keepdims=True), axis=1, keepdims=True) + EPS)
    bank_unit = bank_values * bank_inv
    bank_x[...] = bank_unit
    own_row[...] = bank_x[share].astype(BF16)

    @pl.when(a == 0)
    def _():
        gathered[0, 0, nz // 8, 0] = own_row[...]

    loads[1].wait()
    loads[3].wait()
    loads[4].wait()

    def units(raw):
        values = raw[...].astype(F32)
        inv = 1.0 / jnp.sqrt(jnp.sum(values * values, axis=1, keepdims=True) + EPS)
        return values * inv, inv

    q_unit, q_inv = units(q_raw)
    rows_q[0] = q_unit.astype(BF16)
    meta[0, 0:7, :] = meta_raw[...].astype(F32)
    meta[0, 7:8, :] = w_raw[...]
    loads[2].wait()
    p_unit, p_inv = units(p_raw)
    cols[0:n, :] = p_unit.astype(BF16)

    pl.semaphore_wait(barrier, half // 2 + 2 * a + 2 * (nx - 1) + GROUP - 1)

    def z_copy(k, device):
        return remote(own_row, gathered.at[0, 0, k, a], zf_send.at[k], zf_recv.at[k], device)

    def z_forward(k, carry):
        @pl.when(offset_of(k) != 0)
        def _():
            z_copy(k, up_z(-offset_of(k))).start()

        return carry

    lax.fori_loop(0, half // 2, z_forward, 0)

    sibling = member(1)
    neighbour = member(2)
    partner = member(6)
    to_meta = [send(meta.at[0], meta.at[m], m - 1, member(m)) for m in (1, 2, 3)]
    to_q = send(rows_q.at[0], rows_q.at[2], 3, neighbour)
    to_p = send(cols.at[pl.ds(0, n)], cols.at[pl.ds(n, n)], 4, partner)
    to_q1 = send(rows_q.at[0], rows_q.at[1], 5, sibling)

    def score(ci, s):
        logits = dot_nt(cols[ci * n : (ci + 1) * n, :], rows_q[s]) * HEAT
        e = jnp.exp(logits)
        e_t[ci * n : (ci + 1) * n, s * n : (s + 1) * n] = e
        return logits, jnp.sum(e, axis=0, keepdims=True)

    def z_forward_wait(k, carry):
        @pl.when(offset_of(k) != 0)
        def _():
            z_copy(k, sibling).wait_recv()

        return carry

    plane_order = [(dx, da) for dx in range(nx) for da in range(2) if dx or da]
    plane_order.sort(key=lambda at_: -(min(at_[0], nx - at_[0]) + at_[1]))

    def to_plane(part):
        for dx, da in plane_order:
            if dx:
                yy = y_p if da else y
                send(
                    gathered.at[part, 0, :, a],
                    gathered.at[part, (nx - dx) % nx, :, a],
                    8 + 8 * part + 2 * dx + da,
                    at(z, lax.rem(x + dx, nx), yy, c),
                )
        send(gathered.at[part, 0, :, a], gathered.at[part, 0, :, a], 8 + 8 * part + 1, partner)

    def from_plane(part):
        for dx in range(nx):
            for da, aa in ((0, a), (1, 1 - a)):
                if dx or da:
                    index = 8 + 8 * part + 2 * dx + da
                    landed = gathered.at[part, (nx - dx) % nx, :, aa]
                    remote(landed, landed, send_sem.at[index], recv_sem.at[index], sibling).wait_recv()

    totals = [None] * 4
    logits, totals[0] = score(0, 0)
    eye = lax.broadcasted_iota(jnp.int32, (n, n), 0) == lax.broadcasted_iota(jnp.int32, (n, n), 1)
    positive = jnp.sum(jnp.where(eye, logits, 0.0), axis=0, keepdims=True)
    to_q1.wait_recv()
    totals[1] = score(0, 1)[1]
    lax.fori_loop(0, half // 2, z_forward_wait, 0)
    eighth = nz // 8
    low, high = pl.ds(0, eighth), pl.ds(eighth, eighth)
    to_high = send(gathered.at[0, 0, low, a], gathered.at[1, 0, high, a], 28, up_z(quarter))
    to_low = send(gathered.at[0, 0, high, a], gathered.at[1, 0, low, a], 29, up_z(-quarter))
    to_plane(0)

    to_q.wait_recv()
    to_q3 = send(rows_q.at[2], rows_q.at[3], 6, sibling)
    totals[2] = score(0, 2)[1]
    to_p.wait_recv()
    for s in range(3):
        totals[s] = totals[s] + score(1, s)[1]
    to_q3.wait_recv()
    totals[3] = score(0, 3)[1] + score(1, 3)[1]
    for copy in to_meta:
        copy.wait_recv()

    hb = nb // 2
    all_q = rows_q[...].reshape(4 * n, depth)

    def bank_score(part):
        first = 2 * n + part * hb
        wide[part * hb : (part + 1) * hb] = gathered[part].reshape(hb, groups, lanes).astype(F32)
        for j in range(groups):
            cols[first : first + hb, j * lanes : (j + 1) * lanes] = wide[part * hb : (part + 1) * hb, j, :].astype(BF16)
        e = jnp.exp(dot_nt(cols[first : first + hb, :], all_q) * HEAT)
        e_t[first : first + hb, :] = e
        return [jnp.sum(e[:, s * n : (s + 1) * n] * named[part][s], axis=0, keepdims=True) for s in range(4)]

    named = []
    for part in range(2):
        row = lax.broadcasted_iota(jnp.int32, (hb, n), 0)
        row_z = lax.rem(z + part * half + lax.rem(row, half) - quarter + nz, nz)
        row_x = lax.rem(x + row // half, nx)
        row_id = (4 * (row_z * nx + row_x) + share).astype(F32)
        counts = []
        for s in range(4):
            count = jnp.zeros((hb, n), F32)
            for k in range(7):
                count = count + jnp.where(row_id == meta[s, k : k + 1, :], 1.0, 0.0)
            counts.append(count)
        named.append(counts)

    from_plane(0)
    near = bank_score(0)
    to_high.wait_recv()
    to_low.wait_recv()
    to_plane(1)
    from_plane(1)
    far = bank_score(1)
    for s in range(4):
        sums[0, s : s + 1, :] = totals[s] + near[s] + far[s]

    to_sums = [send(sums.at[0], sums.at[m], 24 + m, member(m)) for m in (2, 3, 1)]
    for copy in to_sums:
        copy.wait_recv()
    coefs, scaled = [], []
    for s in range(4):
        total = sums[0, s : s + 1, :]
        for m in (1, 2, 3):
            total = total + sums[m, s ^ m : (s ^ m) + 1, :]
        if s == 0:
            own_total = total
        weight = meta[s, 7:8, :] * HEAT
        scaled.append(weight)
        coefs.append(weight / total)

    def bank_slopes(part):
        first, rows = 2 * n + part * hb, slice(part * hb, (part + 1) * hb)
        for s in range(4):
            slope = (e_t[first : first + hb, s * n : (s + 1) * n] * coefs[s]).astype(BF16).astype(F32)
            g_t[first : first + hb, s * n : (s + 1) * n] = (slope * named[part][s]).astype(BF16)
        up = dot_nn(g_t[first : first + hb, :], all_q)
        for j in range(groups):
            wide[rows, j, :] = up[:, j * lanes : (j + 1) * lanes]
        bank_out[part] = wide[rows].astype(BF16).reshape(nx, half // 2, 2, groups, lanes)
        copies = []
        for dx, da in plane_order:
            yy, aa = (y_p, 1 - a) if da else (y, a)
            copies.append(
                send(
                    bank_out.at[part, dx, :, aa],
                    plane_in.at[part, da, dx],
                    48 + 8 * part + 2 * dx + da,
                    at(z, lax.rem(x + dx, nx), yy, c),
                )
            )
        return copies

    to_back = [None, bank_slopes(1)]
    to_back[0] = bank_slopes(0)

    loss_out[...] = jnp.log(own_total) - positive

    for s in range(4):
        part = (e_t[n : 2 * n, s * n : (s + 1) * n] * coefs[s]).astype(BF16)
        g_t[n : 2 * n, s * n : (s + 1) * n] = part
    pu_out[...] = dot_nn(g_t[n : 2 * n, :], all_q).astype(BF16)
    for s in range(4):
        part = e_t[0:n, s * n : (s + 1) * n] * coefs[s]
        if s == 0:
            part = part - jnp.where(eye, scaled[0], 0.0)
        g_t[0:n, s * n : (s + 1) * n] = part.astype(BF16)

    def query_part(s):
        return dot_tn(g_t[:, s * n : (s + 1) * n], cols[...])


    def z_back_copy(k, device):
        return remote(z_out.at[k], z_in.at[k], zb_send.at[k], zb_recv.at[k], device)

    def z_back_near(k, carry):
        @pl.when(offset_of(k) != 0)
        def _():
            z_back_copy(k, up_z(offset_of(k))).start()

        return carry

    def bank_reduce(part):
        for copy in to_back[part]:
            copy.wait_recv()
        total = bank_out[part, 0, :, a].astype(F32)
        for dx in range(nx):
            for da in range(2):
                if dx or da:
                    total = total + plane_in[part, da, dx].astype(F32)
        z_out[part * (half // 2) : (part + 1) * (half // 2)] = total.astype(BF16)
        if part:
            for i in range(half // 2):
                k = 3 * nz // 8 + (1 - 2 * (i % 2)) * ((i + 1) // 2)
                z_back_copy(k, up_z(offset_of(k))).start()
        else:
            lax.fori_loop(0, half // 2, z_back_near, 0)

    bank_reduce(1)
    bank_reduce(0)

    @pl.when(a == 0)
    def _():
        z_in[nz // 8] = z_out[nz // 8]

    to_pu = send(pu_out, pu_in, 36, partner)

    qs_out[0] = query_part(3)
    to_qs3 = send(qs_out.at[0], qs_in.at[0], 37, sibling)
    qs_out[1] = query_part(1)
    to_qs1 = send(qs_out.at[1], qs_in.at[1], 38, sibling)
    mine = query_part(2)
    to_qs3.wait_recv()
    qy_out[...] = (mine + qs_in[0]).astype(BF16)
    to_qy = send(qy_out, qy_in, 39, neighbour)
    passage_up = dot_nn(g_t[0:n, :], all_q)
    to_pu.wait_recv()
    passage_up = passage_up + pu_in[...].astype(F32)
    unit, inv = units(p_raw)
    pg_out[...] = inv * (passage_up - unit * jnp.sum(unit * passage_up, axis=1, keepdims=True))
    query_up = query_part(0)
    to_qs1.wait_recv()
    query_up = query_up + qs_in[1]
    to_qy.wait_recv()
    query_up = query_up + qy_in[...].astype(F32)
    unit, inv = units(q_raw)
    qg_out[...] = inv * (query_up - unit * jnp.sum(unit * query_up, axis=1, keepdims=True))

    unit_out[...] = bank_x[...]
    inv_out[...] = jnp.broadcast_to(bank_inv, inv_out.shape)

    for copy in started:
        copy.wait_send()

    def drain(k, carry):
        @pl.when(offset_of(k) != 0)
        def _():
            z_back_copy(k, sibling).wait_send()

        return carry

    def drain_forward(k, carry):
        @pl.when(offset_of(k) != 0)
        def _():
            z_copy(k, sibling).wait_send()

        return carry

    lax.fori_loop(0, half, drain, 0)
    lax.fori_loop(0, half // 2, drain_forward, 0)

    def z_back_wait(k, carry):
        @pl.when(offset_of(k) != 0)
        def _():
            z_back_copy(k, sibling).wait_recv()

        return carry

    lax.fori_loop(0, half, z_back_wait, 0)
    g_in[0] = jnp.sum(z_in[...].astype(F32), axis=0)
    to_all = [send(g_in.at[0], g_in.at[m], 40 + m, member(m)) for m in (5, 4, 7, 6, 3, 2, 1)]
    for copy in to_all:
        copy.wait_recv()
    for delta in range(4):
        first, second = [m for m in range(GROUP) if ROW_OF[m] == delta]
        both = g_in[first] + g_in[second]
        row_b = b if delta < 2 else 1 - b
        row_c = 1 - c if delta & 1 else c
        up_out[2 * row_b + row_c] = both
    for copy in to_all:
        copy.wait_send()


def finish(loss, qg, pg, up_ref, unit_ref, inv_ref, loss_out, qg_out, pg_out, bg_out, slabs, rows, sems):
    copies = [pltpu.make_async_copy(loss, loss_out, sems.at[0])]
    copies += [pltpu.make_async_copy(qg, qg_out, sems.at[1]), pltpu.make_async_copy(pg, pg_out, sems.at[2])]
    for copy in copies:
        copy.start()
    up, unit = up_ref[...], unit_ref[...]
    along = jnp.sum(jnp.sum(unit * up, axis=2, keepdims=True), axis=1, keepdims=True)
    slabs[...] = inv_ref[...] * (up - unit * along)
    for j in range(slabs.shape[1]):
        rows[:, j * 128 : (j + 1) * 128] = slabs[:, j, :]
    last = pltpu.make_async_copy(rows, bg_out, sems.at[3])
    last.start()
    for copy in copies:
        copy.wait()
    last.wait()


def solution(mesh):
    reps = mesh.shape["rep"]
    nx = NX
    nz = reps // nx

    def body(queries, passages, bank, hard_ids, weights):
        n, depth = queries.shape
        nb = reps
        half = nz // 2
        slab = (depth // 128, 128)
        hbm = pl.BlockSpec(memory_space=pltpu.HBM)
        vmem = pl.BlockSpec(memory_space=pltpu.VMEM)
        dma = pltpu.SemaphoreType.DMA
        results = (
            jax.ShapeDtypeStruct((1, n), F32),
            jax.ShapeDtypeStruct((n, depth), F32),
            jax.ShapeDtypeStruct((n, depth), F32),
        )
        small = jax.ShapeDtypeStruct((4,) + slab, F32)
        given = [
            pltpu.with_memory_space_constraint(value, pltpu.HBM)
            for value in (queries, passages, bank, hard_ids.T, weights.reshape(1, n))
        ]
        made = pl.pallas_call(
            functools.partial(kernel, nz, nx),
            out_shape=results + (small,) * 3,
            in_specs=[hbm] * 5,
            out_specs=(vmem,) * 6,
            scratch_shapes=[
                pltpu.VMEM((n, depth), BF16),
                pltpu.VMEM((n, depth), BF16),
                pltpu.VMEM((4, depth), BF16),
                pltpu.VMEM((7, n), jnp.int32),
                pltpu.VMEM((1, n), F32),
                pltpu.VMEM((4, n, depth), BF16),
                pltpu.VMEM((2 * n + nb, depth), BF16),
                pltpu.VMEM((4,) + slab, F32),
                pltpu.VMEM(slab, BF16),
                pltpu.VMEM((2, nx, half // 2, 2) + slab, BF16),
                pltpu.VMEM((nb,) + slab, F32),
                pltpu.VMEM((4, 8, n), F32),
                pltpu.VMEM((4, 8, n), F32),
                pltpu.VMEM((2 * n + nb, 4 * n), F32),
                pltpu.VMEM((2 * n + nb, 4 * n), BF16),
                pltpu.VMEM((2, nx, half // 2, 2) + slab, BF16),
                pltpu.VMEM((2, 2, nx, half // 2) + slab, BF16),
                pltpu.VMEM((half,) + slab, BF16),
                pltpu.VMEM((half,) + slab, BF16),
                pltpu.VMEM((GROUP,) + slab, F32),
                pltpu.VMEM((n, depth), BF16),
                pltpu.VMEM((n, depth), BF16),
                pltpu.VMEM((2, n, depth), F32),
                pltpu.VMEM((2, n, depth), F32),
                pltpu.VMEM((n, depth), BF16),
                pltpu.VMEM((n, depth), BF16),
                dma((5,)),
                dma((64,)),
                dma((64,)),
                dma((half // 2,)),
                dma((half // 2,)),
                dma((half,)),
                dma((half,)),
            ],
            compiler_params=pltpu.CompilerParams(
                collective_id=0, has_side_effects=True, vmem_limit_bytes=40 << 20
            ),
        )(*given)
        losses, query_grad, passage_grad, bank_grad = pl.pallas_call(
            finish,
            out_shape=results + (jax.ShapeDtypeStruct((4, depth), F32),),
            in_specs=[vmem] * 6,
            out_specs=(hbm,) * 4,
            scratch_shapes=[pltpu.VMEM((4,) + slab, F32), pltpu.VMEM((4, depth), F32), dma((4,))],
            compiler_params=pltpu.CompilerParams(vmem_limit_bytes=1 << 20),
        )(*made)
        return losses.reshape(n), query_grad, passage_grad, bank_grad

    placed = (
        P(("grp", "rep"), None),
        P(("grp", "rep"), None),
        P("rep", None),
        P(("grp", "rep"), None),
        P(("grp", "rep")),
    )
    return jax.shard_map(
        body,
        mesh=mesh,
        in_specs=placed,
        out_specs=(
            P(("grp", "rep")),
            P(("grp", "rep"), None),
            P(("grp", "rep"), None),
            P("rep", None),
        ),
        check_vma=False,
    )
```
